512 devices in a mesh: seq: 128 (over y, x, z_hi, core), dp: 4 (over z_lo).
Axes of the slice: x: 4, y: 8, z: 8 (z_hi: 2, z_lo: 4; z = z_hi * 4 + z_lo), core: 2. Of those that a mesh axis runs over, the one named last changes fastest.
Arguments:
- teacher_video: bfloat16 [4, 3, 16384, 1536], P('dp', None, 'seq'), may hold values from -150 to 150
- student_video: bfloat16 [4, 3, 16384, 1536], P('dp', None, 'seq'), may hold values from -150 to 150
- teacher_audio: bfloat16 [4, 2, 4096, 1536], P('dp', None, 'seq'), may hold values from -5 to 5
- student_audio: bfloat16 [4, 2, 4096, 1536], P('dp', None, 'seq'), may hold values from -5 to 5
- alignment: int32 [4, 128, 2], P('dp', 'seq'), may hold values from 0 to 127, as said below
- guidance_index: int32 [4], P('dp'), may hold values from 0 to 7
- step_index: int32 [4], P('dp'), may hold values from 0 to 999
- null_flag: int32 [4], P('dp'), may hold values from 0 to 1, as said below
- gamma: float32 [8, 12], replicated, may hold values from -0.5 to 0.5
Outputs:
- grad_video: bfloat16 [4, 3, 16384, 1536], P('dp', None, 'seq')
- grad_audio: bfloat16 [4, 2, 4096, 1536], P('dp', None, 'seq')
- gamma_grad: float32 [8, 12], replicated
The draws below stay inside these ranges and needn't reach their ends.
Inputs may be any that keep to these rules, and one draw needn't show every extreme that they name: For video block i, alignment[b, i] holds the first audio block s and the number c >= 1 of consecutive audio blocks that intersect it in time; blocks s to s + c - 1 lie inside the clip and within 3 blocks of audio block i. `null_flag`: at least one clip is dropped and at least one is kept.
All inputs are finite; a program needn't handle non-finite values.
Results may differ from the reference program's by a relative error of at most 0.013.
Values may be sent and summed in bfloat16 or wider, within the bound.
No kernel may reach another device: no remote copies, remote signals or barrier semaphores. Data moves between devices by JAX's collectives and lax.ppermute only.
A program may use at most 64 MiB of HBM per device.

```python
import jax
import jax.numpy as jnp
from jax import lax

HEADS = 12
HEAD_DIM = 128
TV = 128
TA = 32
VB = 128
REACH = 3
GLEVELS = 8
CLIPS = 4
NV = 16384
NA = 4096
NVB = 128


def video_draw(key):
    feature_width = HEADS * HEAD_DIM
    shape = (CLIPS, NV, feature_width)
    pieces = jax.random.split(key, 3)
    query = jnp.clip(jax.random.normal(pieces[0], shape, jnp.float32), -5.0, 5.0)
    keys_drawn = jnp.clip(jax.random.normal(pieces[1], shape, jnp.float32), -5.0, 5.0)
    values = jnp.clip(jax.random.normal(pieces[2], shape, jnp.float32), -5.0, 5.0)
    return jnp.clip(jnp.stack([query, keys_drawn, values], axis=1), -150.0, 150.0).astype(jnp.bfloat16)


def draw_teacher_video(key, part):
    return video_draw(jax.random.fold_in(key, 11))


def draw_student_video(key, part):
    return video_draw(jax.random.fold_in(key, 23))


def draw_alignment(key, part):
    owners = NV // TV
    per_device = TV // VB
    blocks = jnp.arange(NVB, dtype=jnp.int32)
    center = blocks // per_device
    low_edge = jnp.maximum(0, center - REACH)
    high_edge = jnp.minimum(owners - 1, center + REACH)
    avail = high_edge - low_edge + 1
    random_ints = jax.random.randint(jax.random.fold_in(key, 37), (CLIPS, NVB, 2), 0, 840, jnp.int32)
    block_count = 1 + random_ints[..., 0] % avail
    block_count = jnp.where(blocks % 16 == 0, avail, block_count)
    first_block = low_edge + random_ints[..., 1] % (avail - block_count + 1)
    return jnp.stack([first_block, block_count], axis=-1).astype(jnp.int32)


def draw_null_flag(key, part):
    pieces = jax.random.split(jax.random.fold_in(key, 53), 2)
    flags = jax.random.randint(pieces[0], (CLIPS,), 0, 2, jnp.int32)
    chosen = jax.random.randint(pieces[1], (), 0, CLIPS, jnp.int32)
    slots = jnp.arange(CLIPS, dtype=jnp.int32)
    flags = jnp.where(slots == chosen, 1, flags)
    flags = jnp.where(slots == (chosen + 1) % CLIPS, 0, flags)
    return flags.astype(jnp.int32)


def plant(values, key, least, largest):
    index_at = [jax.random.randint(jax.random.fold_in(key, axis), (), 0, length) for axis, length in enumerate(values.shape)]
    widest = values.shape.index(max(values.shape))
    beside = index_at[:widest] + [(index_at[widest] + 1) % values.shape[widest]] + index_at[widest + 1:]
    return values.at[tuple(index_at)].set(least).at[tuple(beside)].set(largest)


def shard_levels(rng, dims, cuts, low, high):
    gain = 1.0
    for axis_at, blocks in cuts:
        draws = jax.random.uniform(jax.random.fold_in(jax.random.fold_in(rng, 6), axis_at), (blocks,), jnp.float32, low / len(cuts), high / len(cuts))
        gain = gain * jnp.repeat(jnp.exp(draws), dims[axis_at] // blocks).reshape((-1,) + (1,) * (len(dims) - 1 - axis_at))
    return gain


def gaussian(own_key, extent, deviation, limit, shards=(), kind=jnp.bfloat16):
    result = jax.random.normal(own_key, extent, jnp.float32) * deviation
    if len(shards) > 0:
        result = shard_levels(own_key, extent, shards, -0.22, 0.18) * result
    return jnp.clip(result, min=-limit, max=limit).astype(kind)


def setup_inputs(seed: int = 0) -> dict:
    splits = jax.random.split(jax.random.key(seed), 10)
    return {
        "teacher_video": draw_teacher_video(jax.random.fold_in(splits[9], 71), 0),
        "student_video": draw_student_video(jax.random.fold_in(splits[9], 71), 0),
        "teacher_audio": gaussian(splits[2], (CLIPS, 2, NA, HEADS * HEAD_DIM), 1.0, 5.0, ((0, 4), (2, 128))),
        "student_audio": gaussian(splits[3], (CLIPS, 2, NA, HEADS * HEAD_DIM), 1.0, 5.0, ((0, 4), (2, 128))),
        "alignment": draw_alignment(jax.random.fold_in(splits[9], 71), 0),
        "guidance_index": plant(jax.random.randint(splits[5], (CLIPS,), 0, GLEVELS), jax.random.fold_in(splits[5], 1), 0, GLEVELS - 1).astype(jnp.int32),
        "step_index": plant(jax.random.randint(splits[6], (CLIPS,), 0, 1000), jax.random.fold_in(splits[6], 1), 0, 999).astype(jnp.int32),
        "null_flag": draw_null_flag(jax.random.fold_in(splits[9], 71), 0),
        "gamma": jnp.clip(jax.random.uniform(splits[8], (GLEVELS, HEADS), jnp.float32, -0.5, 0.5), -0.5, 0.5),
    }


def as_float(array):
    return array.astype(jnp.float32)


def joint_probs(scores, usable):
    masked = jnp.where(usable, scores, -jnp.inf)
    highest = jnp.max(masked, axis=-1, keepdims=True)
    exponent = jnp.exp(masked - highest)
    return exponent / jnp.sum(exponent, axis=-1, keepdims=True)


def reference(teacher_video, student_video, teacher_audio, student_audio, alignment, guidance_index, step_index, null_flag, gamma):
    feature_width = HEADS * HEAD_DIM
    window = (2 * REACH + 1) * TA
    score_scale = HEAD_DIM ** -0.5
    levels = jnp.arange(GLEVELS, dtype=jnp.int32)
    video_list = []
    audio_list = []
    gamma_total = jnp.zeros((GLEVELS, HEADS), jnp.float32)
    for clip_index in range(CLIPS):
        level_index = guidance_index[clip_index]
        weight = 1.0 + 0.75 * level_index.astype(jnp.float32)
        loss_weight = 1.0 / (1.0 + step_index[clip_index].astype(jnp.float32) / 250.0)
        keep_audio = null_flag[clip_index] == 0
        factor = jnp.sum(jnp.where(levels[:, None] == level_index, gamma, jnp.zeros_like(gamma)), axis=0)
        teacher_pad = jnp.pad(teacher_audio[clip_index], ((0, 0), (0, window), (0, 0)))
        student_pad = jnp.pad(student_audio[clip_index], ((0, 0), (0, window), (0, 0)))
        teach_clip = teacher_video[clip_index]
        pupil_clip = student_video[clip_index]

        def advance(carried, block_index):
            audio_sums, head_totals = carried
            first_block = alignment[clip_index, block_index, 0].astype(jnp.int32)
            block_count = alignment[clip_index, block_index, 1].astype(jnp.int32)
            offset = (block_index * VB).astype(jnp.int32)
            teach_vid = lax.dynamic_slice_in_dim(teach_clip, offset, VB, 1).reshape(3, VB, HEADS, HEAD_DIM)
            pupil_vid = lax.dynamic_slice_in_dim(pupil_clip, offset, VB, 1).reshape(3, VB, HEADS, HEAD_DIM)
            low_edge = (first_block * TA).astype(jnp.int32)
            teach_aud = lax.dynamic_slice_in_dim(teacher_pad, low_edge, window, 1).reshape(2, window, HEADS, HEAD_DIM)
            pupil_aud = lax.dynamic_slice_in_dim(student_pad, low_edge, window, 1).reshape(2, window, HEADS, HEAD_DIM)
            audio_ok = ((jnp.arange(window, dtype=jnp.int32) // TA) < block_count) & keep_audio
            usable = jnp.concatenate([jnp.ones((VB,), bool), audio_ok])[None, None, :]
            teach_keys = jnp.concatenate([teach_vid[1], teach_aud[0]], axis=0)
            teach_values = jnp.concatenate([teach_vid[2], teach_aud[1]], axis=0)
            teach_scores = jnp.einsum("qhe,khe->hqk", as_float(teach_vid[0]), as_float(teach_keys)) * score_scale
            cond_probs = joint_probs(teach_scores, usable).astype(jnp.bfloat16)
            conditional = jnp.einsum("hqk,khe->qhe", as_float(cond_probs), as_float(teach_values))
            plain_probs = joint_probs(teach_scores[..., :VB], jnp.ones((1, 1, VB), bool)).astype(jnp.bfloat16)
            unconditional = jnp.einsum("hqk,khe->qhe", as_float(plain_probs), as_float(teach_vid[2]))
            target = unconditional + weight * (conditional - unconditional)
            pupil_query = pupil_vid[0]
            pupil_keys = jnp.concatenate([pupil_vid[1], pupil_aud[0]], axis=0)
            pupil_values = jnp.concatenate([pupil_vid[2], pupil_aud[1]], axis=0)
            pupil_scores = jnp.einsum("qhe,khe->hqk", as_float(pupil_query), as_float(pupil_keys)) * score_scale
            probs = joint_probs(pupil_scores, usable)
            probs_round = probs.astype(jnp.bfloat16)
            student_out = jnp.einsum("hqk,khe->qhe", as_float(probs_round), as_float(pupil_values))
            residual = loss_weight * (student_out * factor[None, :, None] - target)
            head_sums = jnp.sum(residual * student_out, axis=(0, 2))
            out_grad = (residual * factor[None, :, None]).astype(jnp.bfloat16)
            prob_grad = jnp.einsum("qhe,khe->hqk", as_float(out_grad), as_float(pupil_values))
            row_delta = jnp.sum(as_float(out_grad) * student_out, axis=-1)
            score_grad = (score_scale * probs * (prob_grad - jnp.transpose(row_delta)[:, :, None])).astype(jnp.bfloat16)
            query_grad = jnp.einsum("hqk,khe->qhe", as_float(score_grad), as_float(pupil_keys))
            key_grad = jnp.einsum("hqk,qhe->khe", as_float(score_grad), as_float(pupil_query))
            value_grad = jnp.einsum("hqk,qhe->khe", as_float(probs_round), as_float(out_grad))
            video_grad = jnp.stack([query_grad, key_grad[:VB], value_grad[:VB]]).reshape(3, VB, feature_width).astype(jnp.bfloat16)
            audio_grad = jnp.stack([key_grad[VB:], value_grad[VB:]]).reshape(2, window, feature_width)
            placed = lax.dynamic_slice_in_dim(audio_sums, low_edge, window, 1) + audio_grad
            audio_sums = lax.dynamic_update_slice_in_dim(audio_sums, placed, low_edge, 1)
            return (audio_sums, head_totals + head_sums), video_grad

        initial = (jnp.zeros((2, NA + window, feature_width), jnp.float32), jnp.zeros((HEADS,), jnp.float32))
        (audio_sums, head_totals), video_blocks = lax.scan(advance, initial, jnp.arange(NVB, dtype=jnp.int32))
        video_list.append(jnp.transpose(video_blocks, (1, 0, 2, 3)).reshape(3, NV, feature_width))
        audio_list.append(audio_sums[:, :NA].astype(jnp.bfloat16))
        gamma_total = gamma_total + jnp.where(levels[:, None] == level_index, head_totals[None, :], jnp.zeros_like(gamma_total))
    return jnp.stack(video_list), jnp.stack(audio_list), gamma_total / (NV * HEAD_DIM)
```

```python
import functools

import jax
import jax.numpy as jnp
from jax import lax
from jax.experimental import pallas as pl
from jax.experimental.pallas import tpu as pltpu
from jax.sharding import Mesh
from jax.sharding import PartitionSpec as P

SEQ = ("seq_0", "seq_1", "seq_2", "seq_3")
PLANE = ("seq_0", "seq_1")
COLUMN = ("seq_2", "seq_3", "dp")
HALF = "seq_2"
CORE = "seq_3"
SLOTS = 8
STEP_HEADS = 2
VMEM = 28 * 1024 * 1024


def dot(a, b, contract_a, contract_b):
    return lax.dot_general(
        a, b, (((contract_a,), (contract_b,)), ((), ())), preferred_element_type=jnp.float32
    )


def by_block(f, *pairs):
    return jnp.concatenate([f(*args) for args in zip(*pairs)], axis=1)


def halves(x):
    n = x.shape[1] // 2
    return x[:, :n], x[:, n:]


def with_bias(scores, bias, rows):
    out = []
    for slot in range(SLOTS):
        piece = halves(scores[slot * rows : (slot + 1) * rows])
        out.append(jnp.concatenate([piece[b] + bias[2 * slot + b] for b in range(2)], axis=1))
    return jnp.concatenate(out, axis=0)


def load_head(lanes, mine, other, audio):
    q = (mine[0, 0, :, lanes], other[0, :, lanes])
    k = (mine[0, 1, :, lanes], other[1, :, lanes])
    v = (mine[0, 2, :, lanes], other[2, :, lanes])
    ka = jnp.concatenate([ref[b, 0, :, lanes] for ref in audio for b in range(2)], axis=0)
    va = jnp.concatenate([ref[b, 1, :, lanes] for ref in audio for b in range(2)], axis=0)
    return q, k, v, ka, va


def scores_of(q, k, ka, scale, bias, rows):
    local = by_block(lambda kb, qb: dot(kb, qb, 1, 1), k, q) * scale
    audio = dot(ka, jnp.concatenate(q, axis=0), 1, 1) * scale
    return local, with_bias(audio, bias, rows)


def column_max(x):
    return jnp.max(x, axis=0, keepdims=True)


def column_sum(x):
    return jnp.sum(x, axis=0, keepdims=True)


def times_values(v, va, local, audio):
    return by_block(lambda vb, pb: dot(vb, pb, 0, 0), v, halves(local)) + dot(va, audio, 0, 0)


def teacher_kernel(dim, core, bias, scal, mine, other, own, zed, far, nat, target):
    rows = own.shape[2]
    for i in range(target.shape[0]):
        lanes = slice(i * dim, (i + 1) * dim)
        q, k, v, ka, va = load_head(lanes, mine, other, (own, zed, far, nat))
        local, audio = scores_of(q, k, ka, dim**-0.5, bias, rows)
        plain_max = column_max(local)
        plain = jnp.exp(local - plain_max)
        plain = (plain * (1.0 / column_sum(plain))).astype(jnp.bfloat16)
        highest = jnp.maximum(plain_max, column_max(audio))
        local = jnp.exp(local - highest)
        audio = jnp.exp(audio - highest)
        norm = 1.0 / (column_sum(local) + column_sum(audio))
        local = (local * norm).astype(jnp.bfloat16)
        audio = (audio * norm).astype(jnp.bfloat16)
        conditional = times_values(v, va, local, audio)
        unconditional = by_block(lambda vb, pb: dot(vb, pb, 0, 0), v, halves(plain))
        target[i] = unconditional + scal[0] * (conditional - unconditional)


def student_kernel(
    dim,
    core,
    bias,
    scal,
    mine,
    other,
    own,
    zed,
    far,
    nat,
    target,
    grad_mine,
    grad_other,
    own_out,
    zed_out,
    far_out,
    nat_out,
    totals,
):
    rows = own.shape[2]
    scale = dim**-0.5
    heads = target.shape[0]
    for i in range(heads):
        lanes = slice(i * dim, (i + 1) * dim)
        q, k, v, ka, va = load_head(lanes, mine, other, (own, zed, far, nat))
        local, audio = scores_of(q, k, ka, scale, bias, rows)
        highest = jnp.maximum(column_max(local), column_max(audio))
        local = jnp.exp(local - highest)
        audio = jnp.exp(audio - highest)
        norm = 1.0 / (column_sum(local) + column_sum(audio))
        local = local * norm
        audio = audio * norm
        local_round = local.astype(jnp.bfloat16)
        audio_round = audio.astype(jnp.bfloat16)
        out = times_values(v, va, local_round, audio_round)
        factor = scal[2 + pl.program_id(0) * heads + i]
        residual = scal[1] * (out * factor - target[i])
        product = residual * out
        n = product.shape[1] // 2
        product = product[:, :n] + product[:, n:]
        totals[i] = jnp.sum(product.reshape(dim // 8, 8, n), axis=0)
        out_grad = (residual * factor).astype(jnp.bfloat16)
        row_delta = column_sum(out_grad.astype(jnp.float32) * out)
        grads = halves(out_grad)
        local_grad = by_block(lambda vb, gb: dot(vb, gb, 1, 0), v, grads)
        audio_grad = dot(va, out_grad, 1, 0)
        local_grad = (scale * local * (local_grad - row_delta)).astype(jnp.bfloat16)
        audio_grad = (scale * audio * (audio_grad - row_delta)).astype(jnp.bfloat16)
        query_grad = times_values(k, ka, local_grad, audio_grad).T.astype(jnp.bfloat16)
        vb = query_grad.shape[0] // 2
        score_halves = halves(local_grad)
        prob_halves = halves(local_round)
        for b, ref in enumerate((grad_mine, grad_other)):
            ref[0, :, lanes] = query_grad[b * vb : (b + 1) * vb]
            ref[1, :, lanes] = dot(score_halves[b], q[b], 1, 0).astype(jnp.bfloat16)
            ref[2, :, lanes] = dot(prob_halves[b], grads[b], 1, 1).astype(jnp.bfloat16)
        audio_keys = dot(audio_grad, jnp.concatenate(q, axis=0), 1, 0)
        audio_values = dot(audio_round, out_grad, 1, 1)
        for slot in range(SLOTS):
            ref = (own_out, zed_out, far_out, nat_out)[slot // 2]
            at = slice(slot * rows, (slot + 1) * rows)
            ref[slot % 2, 0, :, lanes] = audio_keys[at].astype(ref.dtype)
            ref[slot % 2, 1, :, lanes] = audio_values[at].astype(ref.dtype)


def specs(steps, width, vb, rows):
    smem = pl.BlockSpec(memory_space=pltpu.SMEM)
    mine = pl.BlockSpec((1, 3, vb, width), lambda h, c: (0, 0, 0, c[0] * steps + h))
    video = pl.BlockSpec((3, vb, width), lambda h, c: (0, 0, h))
    window = pl.BlockSpec((2, 2, rows, width), lambda h, c: (0, 0, 0, c[0] * steps + h))
    piece = pl.BlockSpec((2, 2, rows, width), lambda h, c: (0, 0, 0, h))
    return smem, mine, video, window, piece


def teacher_call(core, bias, scal, mine, other, audio, head_dim):
    vb, half_width = mine.shape[2], other.shape[2]
    rows = audio[0].shape[2]
    width = STEP_HEADS * head_dim
    steps = half_width // width
    smem, own_video, video, window, _ = specs(steps, width, vb, rows)
    heads = half_width // head_dim
    return pl.pallas_call(
        functools.partial(teacher_kernel, head_dim),
        grid_spec=pltpu.PrefetchScalarGridSpec(
            num_scalar_prefetch=1,
            grid=(steps,),
            in_specs=[smem, smem, own_video, video] + [window] * 4,
            out_specs=pl.BlockSpec((STEP_HEADS, head_dim, 2 * vb), lambda h, c: (h, 0, 0)),
        ),
        out_shape=jax.ShapeDtypeStruct((heads, head_dim, 2 * vb), jnp.float32),
        compiler_params=pltpu.CompilerParams(vmem_limit_bytes=VMEM),
        cost_estimate=pl.CostEstimate(
            flops=600_000_000, bytes_accessed=4_000_000, transcendentals=900_000
        ),
        name="teacher",
    )(core, bias, scal, mine, other, *audio)


def student_call(core, bias, scal, mine, other, audio, target, head_dim):
    vb, half_width = mine.shape[2], other.shape[2]
    rows = audio[0].shape[2]
    width = STEP_HEADS * head_dim
    steps = half_width // width
    smem, own_video, video, window, piece = specs(steps, width, vb, rows)
    heads = half_width // head_dim
    video_shape = jax.ShapeDtypeStruct((3, vb, half_width), jnp.bfloat16)
    wide = jax.ShapeDtypeStruct((2, 2, rows, half_width), jnp.float32)
    narrow = jax.ShapeDtypeStruct((2, 2, rows, half_width), jnp.bfloat16)
    return pl.pallas_call(
        functools.partial(student_kernel, head_dim),
        grid_spec=pltpu.PrefetchScalarGridSpec(
            num_scalar_prefetch=1,
            grid=(steps,),
            in_specs=[smem, smem, own_video, video]
            + [window] * 4
            + [pl.BlockSpec((STEP_HEADS, head_dim, 2 * vb), lambda h, c: (h, 0, 0))],
            out_specs=[video, video, piece, piece, piece, piece]
            + [pl.BlockSpec((STEP_HEADS, 8, vb), lambda h, c: (h, 0, 0))],
        ),
        out_shape=[video_shape, video_shape, wide, wide, narrow, narrow]
        + [jax.ShapeDtypeStruct((heads, 8, vb), jnp.float32)],
        compiler_params=pltpu.CompilerParams(vmem_limit_bytes=VMEM),
        cost_estimate=pl.CostEstimate(
            flops=900_000_000, bytes_accessed=8_000_000, transcendentals=600_000
        ),
        name="student",
    )(core, bias, scal, mine, other, *audio, target)


def swap(x, axis):
    return lax.ppermute(x, axis, [(0, 1), (1, 0)])


def everywhere(x, axes):
    n = lax.axis_size(axes)
    copies = jnp.broadcast_to(x[None], (n,) + x.shape)
    return jnp.sum(lax.all_to_all(copies, axes, 0, 0), axis=0)


def body(
    teacher_video,
    student_video,
    teacher_audio,
    student_audio,
    alignment,
    guidance_index,
    step_index,
    null_flag,
    gamma,
):
    heads = gamma.shape[1]
    width = teacher_video.shape[3]
    half_width = width // 2
    head_dim = width // heads
    half_heads = heads // 2
    tokens = teacher_video.shape[2]
    core = lax.axis_index(CORE)
    half = lax.axis_index(HALF)
    position = lax.axis_index(SEQ)
    base = position - core

    group = lax.axis_size(HALF) * lax.axis_size(CORE)
    count = lax.axis_size(SEQ)
    places = range(count)

    def inside(pairs):
        return [(a, b) for a, b in pairs if 0 <= b < count]

    near_pairs = inside((i, i + group if i % 2 else i - group) for i in places)
    far_out = inside((i, i - group if (i // 2) % 2 else i + group) for i in places)
    far_back = [(b, a) for a, b in far_out]

    teach, pupil = teacher_audio[0], student_audio[0]
    teach_zed = swap(teach, HALF)
    pupil_zed = swap(pupil, HALF)
    teach_nat = lax.ppermute(teach, SEQ, near_pairs)
    pupil_nat = lax.ppermute(pupil, SEQ, near_pairs)
    teach_far = lax.ppermute(teach_zed, SEQ, far_out)
    pupil_far = lax.ppermute(pupil_zed, SEQ, far_out)

    def sibling(video):
        return swap(lax.dynamic_slice_in_dim(video[0], (1 - core) * half_width, half_width, 2), CORE)

    teach_other = sibling(teacher_video)
    pupil_other = sibling(student_video)
    spans = lax.all_gather(alignment[0, 0], CORE)

    def both(pieces):
        return [lax.all_gather(piece, CORE) for piece in pieces]

    teach_window = both((teach, teach_zed, teach_far, teach_nat))
    pupil_window = both((pupil, pupil_zed, pupil_far, pupil_nat))

    side = 2 - 4 * half
    owners = base + jnp.stack(
        [jnp.int32(0), jnp.int32(1), side, side + 1, -side, 1 - side, jnp.int32(4), jnp.int32(-3)]
    )
    order = jnp.stack([core, 1 - core])
    first = jnp.take(spans[:, 0], order)[None, :]
    length = jnp.take(spans[:, 1], order)[None, :]
    used = (owners[:, None] >= first) & (owners[:, None] < first + length) & (null_flag[0] == 0)
    bias = jnp.where(used, 0.0, -jnp.inf).astype(jnp.float32).reshape(2 * SLOTS)

    level_index = guidance_index[0]
    levels = jnp.arange(gamma.shape[0], dtype=jnp.int32)
    weight = 1.0 + 0.75 * level_index.astype(jnp.float32)
    loss_weight = 1.0 / (1.0 + step_index[0].astype(jnp.float32) / 250.0)
    factor = jnp.sum(
        jnp.where(levels[:, None] == level_index, gamma, jnp.zeros_like(gamma)), axis=0
    )
    factor = lax.dynamic_slice_in_dim(factor, core * half_heads, half_heads)
    scal = jnp.concatenate([jnp.stack([weight, loss_weight]), factor])
    which = core.astype(jnp.int32)[None]

    target = teacher_call(which, bias, scal, teacher_video, teach_other, teach_window, head_dim)
    grad_mine, grad_other, own, zed, far, nat, totals = student_call(
        which, bias, scal, student_video, pupil_other, pupil_window, target, head_dim
    )

    far_in = lax.ppermute(far, SEQ, far_back)
    next_in = lax.ppermute(nat[0], SEQ, inside((i, i + group) for i in places))
    prev_in = lax.ppermute(nat[1], SEQ, inside((i, i - group) for i in places))
    zed_in = swap((zed + far_in.astype(jnp.float32)).astype(jnp.bfloat16), HALF)
    own = own + zed_in.astype(jnp.float32)
    own = own + jnp.stack([next_in, prev_in]).astype(jnp.float32)
    leave = lax.dynamic_index_in_dim(own, 1 - core, 0, keepdims=False).astype(jnp.bfloat16)
    keep = lax.dynamic_index_in_dim(own, core, 0, keepdims=False).astype(jnp.bfloat16)

    def joined(mine, other):
        return jnp.where(
            core == 0,
            jnp.concatenate([mine, other], axis=-1),
            jnp.concatenate([other, mine], axis=-1),
        )[None]

    grad_audio = joined(keep, swap(leave, CORE))
    grad_video = joined(grad_mine, swap(grad_other, CORE))

    sums = jnp.sum(totals, axis=(1, 2))
    head_totals = lax.dynamic_update_slice_in_dim(
        jnp.zeros((heads,), jnp.float32), sums, core * half_heads, 0
    )
    contribution = jnp.where(
        levels[:, None] == level_index, head_totals[None, :], jnp.zeros_like(gamma)
    )
    gamma_grad = everywhere(everywhere(contribution, COLUMN), PLANE) / (tokens * count * head_dim)
    return (grad_video, grad_audio, gamma_grad)


def solution(mesh):
    finer = Mesh(
        mesh.devices.reshape(8, 4, 2, 2, mesh.shape["dp"]),
        ("seq_0", "seq_1", "seq_2", "seq_3", "dp"),
    )
    in_specs = (
        P("dp", None, SEQ, None),
        P("dp", None, SEQ, None),
        P("dp", None, SEQ, None),
        P("dp", None, SEQ, None),
        P("dp", SEQ, None),
        P("dp"),
        P("dp"),
        P("dp"),
        P(),
    )
    out_specs = (P("dp", None, SEQ, None), P("dp", None, SEQ, None), P())
    return jax.shard_map(body, mesh=finer, in_specs=in_specs, out_specs=out_specs, check_vma=False)
```

```python
import functools

import jax
import jax.numpy as jnp
from jax import lax
from jax.experimental import pallas as pl
from jax.experimental.pallas import tpu as pltpu
from jax.sharding import Mesh
from jax.sharding import PartitionSpec as P

SEQ = ("seq_0", "seq_1", "seq_2", "seq_3")
PLANE = ("seq_0", "seq_1")
COLUMN = ("seq_2", "seq_3", "dp")
HALF = "seq_2"
CORE = "seq_3"
SLOTS = 8
STEP_HEADS = 2
VMEM = 28 * 1024 * 1024


def dot(a, b, contract_a, contract_b):
    return lax.dot_general(
        a, b, (((contract_a,), (contract_b,)), ((), ())), preferred_element_type=jnp.float32
    )


def by_block(f, *pairs):
    return jnp.concatenate([f(*args) for args in zip(*pairs)], axis=1)


def halves(x):
    n = x.shape[1] // 2
    return x[:, :n], x[:, n:]


def with_bias(scores, bias, rows):
    out = []
    for slot in range(SLOTS):
        piece = halves(scores[slot * rows : (slot + 1) * rows])
        out.append(jnp.concatenate([piece[b] + bias[2 * slot + b] for b in range(2)], axis=1))
    return jnp.concatenate(out, axis=0)


def load_head(lanes, mine, other, audio):
    q = (mine[0, 0, :, lanes], other[0, :, lanes])
    k = (mine[0, 1, :, lanes], other[1, :, lanes])
    v = (mine[0, 2, :, lanes], other[2, :, lanes])
    own, zed, far, same, opposite = audio

    def window(i):
        pieces = [ref[b, i, :, lanes] for ref in (own, zed, far) for b in range(2)]
        return jnp.concatenate(pieces + [same[i, :, lanes], opposite[i, :, lanes]], axis=0)

    return q, k, v, window(0), window(1)


def scores_of(q, k, ka, scale, bias, rows):
    local = by_block(lambda kb, qb: dot(kb, qb, 1, 1), k, q) * scale
    audio = dot(ka, jnp.concatenate(q, axis=0), 1, 1) * scale
    return local, with_bias(audio, bias, rows)


def column_max(x):
    return jnp.max(x, axis=0, keepdims=True)


def column_sum(x):
    return jnp.sum(x, axis=0, keepdims=True)


def times_values(v, va, local, audio):
    return by_block(lambda vb, pb: dot(vb, pb, 0, 0), v, halves(local)) + dot(va, audio, 0, 0)


def teacher_kernel(dim, core, bias, scal, mine, other, own, zed, far, same, opposite, target):
    rows = own.shape[2]
    for i in range(target.shape[0]):
        lanes = slice(i * dim, (i + 1) * dim)
        q, k, v, ka, va = load_head(lanes, mine, other, (own, zed, far, same, opposite))
        local, audio = scores_of(q, k, ka, dim**-0.5, bias, rows)
        plain_max = column_max(local)
        plain = jnp.exp(local - plain_max)
        plain = (plain * (1.0 / column_sum(plain))).astype(jnp.bfloat16)
        highest = jnp.maximum(plain_max, column_max(audio))
        local = jnp.exp(local - highest)
        audio = jnp.exp(audio - highest)
        norm = 1.0 / (column_sum(local) + column_sum(audio))
        local = (local * norm).astype(jnp.bfloat16)
        audio = (audio * norm).astype(jnp.bfloat16)
        conditional = times_values(v, va, local, audio)
        unconditional = by_block(lambda vb, pb: dot(vb, pb, 0, 0), v, halves(plain))
        target[i] = unconditional + scal[0] * (conditional - unconditional)


def student_kernel(
    dim,
    core,
    bias,
    scal,
    mine,
    other,
    own,
    zed,
    far,
    same,
    opposite,
    target,
    grad_mine,
    grad_other,
    own_out,
    zed_out,
    far_out,
    opposite_out,
    totals,
):
    rows = own.shape[2]
    scale = dim**-0.5
    heads = target.shape[0]
    for i in range(heads):
        lanes = slice(i * dim, (i + 1) * dim)
        q, k, v, ka, va = load_head(lanes, mine, other, (own, zed, far, same, opposite))
        local, audio = scores_of(q, k, ka, scale, bias, rows)
        highest = jnp.maximum(column_max(local), column_max(audio))
        local = jnp.exp(local - highest)
        audio = jnp.exp(audio - highest)
        norm = 1.0 / (column_sum(local) + column_sum(audio))
        local = local * norm
        audio = audio * norm
        local_round = local.astype(jnp.bfloat16)
        audio_round = audio.astype(jnp.bfloat16)
        out = times_values(v, va, local_round, audio_round)
        factor = scal[2 + pl.program_id(0) * heads + i]
        residual = scal[1] * (out * factor - target[i])
        product = residual * out
        n = product.shape[1] // 2
        product = product[:, :n] + product[:, n:]
        totals[i] = jnp.sum(product.reshape(dim // 8, 8, n), axis=0)
        out_grad = (residual * factor).astype(jnp.bfloat16)
        row_delta = column_sum(out_grad.astype(jnp.float32) * out)
        grads = halves(out_grad)
        local_grad = by_block(lambda vb, gb: dot(vb, gb, 1, 0), v, grads)
        audio_grad = dot(va, out_grad, 1, 0)
        local_grad = (scale * local * (local_grad - row_delta)).astype(jnp.bfloat16)
        audio_grad = (scale * audio * (audio_grad - row_delta)).astype(jnp.bfloat16)
        query_grad = times_values(k, ka, local_grad, audio_grad).T.astype(jnp.bfloat16)
        vb = query_grad.shape[0] // 2
        score_halves = halves(local_grad)
        prob_halves = halves(local_round)
        for b, (ref, first) in enumerate(((grad_mine, (0,)), (grad_other, ()))):
            ref[(*first, 0, slice(None), lanes)] = query_grad[b * vb : (b + 1) * vb]
            key_grad = dot(score_halves[b], q[b], 1, 0)
            ref[(*first, 1, slice(None), lanes)] = key_grad.astype(jnp.bfloat16)
            value_grad = dot(prob_halves[b], grads[b], 1, 1)
            ref[(*first, 2, slice(None), lanes)] = value_grad.astype(jnp.bfloat16)
        audio_keys = dot(audio_grad, jnp.concatenate(q, axis=0), 1, 0)
        audio_values = dot(audio_round, out_grad, 1, 1)
        places = [(own_out, 0), (own_out, 1), (zed_out, 0), (zed_out, 1)]
        places += [(far_out, 0), (far_out, 1), (far_out, 2), (opposite_out, 0)]
        for slot, (ref, b) in enumerate(places):
            at = slice(slot * rows, (slot + 1) * rows)
            ref[b, 0, :, lanes] = audio_keys[at].astype(ref.dtype)
            ref[b, 1, :, lanes] = audio_values[at].astype(ref.dtype)


def specs(steps, width, vb, rows, which):
    smem = pl.BlockSpec(memory_space=pltpu.SMEM)
    mine = pl.BlockSpec((1, 3, vb, width), lambda h, c: (0, 0, 0, c[0] * steps + h))
    video = pl.BlockSpec((3, vb, width), lambda h, c: (0, 0, h))
    pair = pl.BlockSpec((2, 2, rows, width), lambda h, c: (0, 0, 0, h))
    single = pl.BlockSpec((2, rows, width), lambda h, c: (which, 0, h))
    return smem, mine, video, pair, single


def teacher_call(core, bias, scal, mine, other, audio, head_dim):
    vb, half_width = mine.shape[2], other.shape[2]
    rows = audio[0].shape[2]
    width = STEP_HEADS * head_dim
    steps = half_width // width
    smem, own_video, video, pair, single = specs(steps, width, vb, rows, 0)
    heads = half_width // head_dim
    return pl.pallas_call(
        functools.partial(teacher_kernel, head_dim),
        grid_spec=pltpu.PrefetchScalarGridSpec(
            num_scalar_prefetch=1,
            grid=(steps,),
            in_specs=[smem, smem, own_video, video] + [pair] * 3 + [single] * 2,
            out_specs=pl.BlockSpec((STEP_HEADS, head_dim, 2 * vb), lambda h, c: (h, 0, 0)),
        ),
        out_shape=jax.ShapeDtypeStruct((heads, head_dim, 2 * vb), jnp.float32),
        compiler_params=pltpu.CompilerParams(vmem_limit_bytes=VMEM),
        cost_estimate=pl.CostEstimate(
            flops=600_000_000, bytes_accessed=4_000_000, transcendentals=900_000
        ),
        name="teacher",
    )(core, bias, scal, mine, other, *audio)


def student_call(core, bias, scal, mine, other, audio, target, head_dim):
    vb, half_width = mine.shape[2], other.shape[2]
    rows = audio[0].shape[2]
    width = STEP_HEADS * head_dim
    steps = half_width // width
    smem, own_video, video, pair, single = specs(steps, width, vb, rows, 1)
    heads = half_width // head_dim

    def blocks(n, dtype):
        shape = jax.ShapeDtypeStruct((n, 2, rows, half_width), dtype)
        return shape, pl.BlockSpec((n, 2, rows, width), lambda h, c: (0, 0, 0, h))

    outs = [
        (jax.ShapeDtypeStruct(mine.shape, jnp.bfloat16), own_video),
        (jax.ShapeDtypeStruct(other.shape, jnp.bfloat16), video),
        blocks(2, jnp.float32),
        blocks(2, jnp.float32),
        blocks(3, jnp.bfloat16),
        blocks(1, jnp.bfloat16),
        (
            jax.ShapeDtypeStruct((heads, 8, vb), jnp.float32),
            pl.BlockSpec((STEP_HEADS, 8, vb), lambda h, c: (h, 0, 0)),
        ),
    ]
    return pl.pallas_call(
        functools.partial(student_kernel, head_dim),
        grid_spec=pltpu.PrefetchScalarGridSpec(
            num_scalar_prefetch=1,
            grid=(steps,),
            in_specs=[smem, smem, own_video, video]
            + [pair] * 3
            + [single] * 2
            + [pl.BlockSpec((STEP_HEADS, head_dim, 2 * vb), lambda h, c: (h, 0, 0))],
            out_specs=[spec for _, spec in outs],
        ),
        out_shape=[shape for shape, _ in outs],
        compiler_params=pltpu.CompilerParams(vmem_limit_bytes=VMEM),
        cost_estimate=pl.CostEstimate(
            flops=900_000_000, bytes_accessed=8_000_000, transcendentals=600_000
        ),
        name="student",
    )(core, bias, scal, mine, other, *audio, target)


def swap(x, axis):
    return lax.ppermute(x, axis, [(0, 1), (1, 0)])


def everywhere(x, axes):
    n = lax.axis_size(axes)
    copies = jnp.broadcast_to(x[None], (n,) + x.shape)
    return jnp.sum(lax.all_to_all(copies, axes, 0, 0), axis=0)


def body(
    teacher_video,
    student_video,
    teacher_audio,
    student_audio,
    alignment,
    guidance_index,
    step_index,
    null_flag,
    gamma,
):
    heads = gamma.shape[1]
    width = teacher_video.shape[3]
    half_width = width // 2
    head_dim = width // heads
    half_heads = heads // 2
    tokens = teacher_video.shape[2]
    core = lax.axis_index(CORE)
    half = lax.axis_index(HALF)
    position = lax.axis_index(SEQ)
    base = position - core

    group = lax.axis_size(HALF) * lax.axis_size(CORE)
    count = lax.axis_size(SEQ)
    places = range(count)

    def inside(pairs):
        return [(a, b) for a, b in pairs if 0 <= b < count]

    far_out = inside((i, i - group if (i // 2) % 2 else i + group) for i in places)
    far_back = [(b, a) for a, b in far_out]

    def part(x, which):
        return lax.dynamic_slice_in_dim(x, which * half_width, half_width, x.ndim - 1)

    audio = jnp.concatenate([teacher_audio[0], student_audio[0]], axis=0)
    got = swap(part(audio, 1 - core), CORE)
    kept = part(audio, core)
    pairs = [jnp.stack([kept[i : i + 2], got[i : i + 2]]) for i in (0, 2)]
    inner = core == half
    zeds = [swap(pair, HALF) for pair in pairs]
    zeds[0], teacher_video, student_video, alignment = lax.optimization_barrier(
        (zeds[0], teacher_video, student_video, alignment)
    )
    same = lax.ppermute(jnp.where(inner, got, kept), SEQ, far_out)
    opposite = lax.ppermute(jnp.where(inner, kept, got), SEQ, far_back)
    fars = [lax.ppermute(zed, SEQ, far_out) for zed in zeds]

    teach_other = swap(part(teacher_video[0], 1 - core), CORE)
    pupil_other = swap(part(student_video[0], 1 - core), CORE)
    spans = lax.all_gather(alignment[0, 0], CORE)

    side = 2 - 4 * half
    near = 7 * half
    owners = jnp.stack(
        [
            base + core,
            base + 1 - core,
            base + side + core,
            base + side + 1 - core,
            base - side + core,
            base - side + 1 - core,
            base - 3 + near,
            base + 4 - near,
        ]
    )
    span = jnp.where(core == 0, spans, spans[::-1])
    first, length = span[None, :, 0], span[None, :, 1]
    used = (owners[:, None] >= first) & (owners[:, None] < first + length) & (null_flag[0] == 0)
    bias = jnp.where(used, 0.0, -jnp.inf).astype(jnp.float32).reshape(2 * SLOTS)

    level_index = guidance_index[0]
    levels = jnp.arange(gamma.shape[0], dtype=jnp.int32)
    weight = 1.0 + 0.75 * level_index.astype(jnp.float32)
    loss_weight = 1.0 / (1.0 + step_index[0].astype(jnp.float32) / 250.0)
    factor = jnp.sum(
        jnp.where(levels[:, None] == level_index, gamma, jnp.zeros_like(gamma)), axis=0
    )
    factor = lax.dynamic_slice_in_dim(factor, core * half_heads, half_heads)
    scal = jnp.concatenate([jnp.stack([weight, loss_weight]), factor])
    which = core.astype(jnp.int32)[None]

    windows = [(pair, zed, far, same, opposite) for pair, zed, far in zip(pairs, zeds, fars)]
    target = teacher_call(which, bias, scal, teacher_video, teach_other, windows[0], head_dim)
    grad_video, grad_other, own, zed, far, opposite, totals = student_call(
        which, bias, scal, student_video, pupil_other, windows[1], target, head_dim
    )

    sums = jnp.sum(totals, axis=(1, 2))
    head_totals = lax.dynamic_update_slice_in_dim(
        jnp.zeros((heads,), jnp.float32), sums, core * half_heads, 0
    )
    contribution = jnp.where(
        levels[:, None] == level_index, head_totals[None, :], jnp.zeros_like(gamma)
    )
    far_in = lax.ppermute(far, SEQ, far_back)
    far_in, contribution = lax.optimization_barrier((far_in, everywhere(contribution, COLUMN)))
    far_in = far_in.astype(jnp.float32)
    opposite_in = lax.ppermute(opposite[0], SEQ, far_out).astype(jnp.float32)
    zed_in = swap((zed + far_in[:2]).astype(jnp.bfloat16), HALF)
    zed_in, gamma_grad = lax.optimization_barrier((zed_in, everywhere(contribution, PLANE)))
    zed_in = zed_in.astype(jnp.float32)
    near_in = (far_in[2], opposite_in)
    keep = own[0] + jnp.where(inner, near_in[1], near_in[0])
    leave = own[1] + jnp.where(inner, near_in[0], near_in[1])
    keep = (keep + zed_in[0]).astype(jnp.bfloat16)
    arrived = swap((leave + zed_in[1]).astype(jnp.bfloat16), CORE)
    grad_audio = jnp.where(
        core == 0,
        jnp.concatenate([keep, arrived], axis=-1),
        jnp.concatenate([arrived, keep], axis=-1),
    )[None]
    grad_video = lax.dynamic_update_slice_in_dim(
        grad_video, swap(grad_other, CORE)[None], (1 - core) * half_width, 3
    )

    gamma_grad = gamma_grad / (tokens * count * head_dim)
    return (grad_video, grad_audio, gamma_grad)


def solution(mesh):
    finer = Mesh(
        mesh.devices.reshape(8, 4, 2, 2, mesh.shape["dp"]),
        ("seq_0", "seq_1", "seq_2", "seq_3", "dp"),
    )
    in_specs = (
        P("dp", None, SEQ, None),
        P("dp", None, SEQ, None),
        P("dp", None, SEQ, None),
        P("dp", None, SEQ, None),
        P("dp", SEQ, None),
        P("dp"),
        P("dp"),
        P("dp"),
        P(),
    )
    out_specs = (P("dp", None, SEQ, None), P("dp", None, SEQ, None), P())
    return jax.shard_map(body, mesh=finer, in_specs=in_specs, out_specs=out_specs, check_vma=False)
```

```python
import functools

import jax
import jax.numpy as jnp
from jax import lax
from jax.experimental import pallas as pl
from jax.experimental.pallas import tpu as pltpu
from jax.sharding import Mesh
from jax.sharding import PartitionSpec as P

SEQ = ("seq_0", "seq_1", "seq_2", "seq_3")
FIRST = ("seq_0", "seq_2")
SECOND = ("seq_1", "dp")
HALF = "seq_2"
CORE = "seq_3"
SLOTS = 8
STEP_HEADS = 3
VMEM = 28 * 1024 * 1024


def dot(a, b, contract_a, contract_b):
    return lax.dot_general(
        a, b, (((contract_a,), (contract_b,)), ((), ())), preferred_element_type=jnp.float32
    )


def by_block(f, *pairs):
    return jnp.concatenate([f(*args) for args in zip(*pairs)], axis=1)


def halves(x):
    n = x.shape[1] // 2
    return x[:, :n], x[:, n:]


def with_bias(scores, bias, rows):
    out = []
    for slot in range(SLOTS):
        piece = halves(scores[slot * rows : (slot + 1) * rows])
        out.append(jnp.concatenate([piece[b] + bias[2 * slot + b] for b in range(2)], axis=1))
    return jnp.concatenate(out, axis=0)


def load_head(lanes, mine, other, audio):
    q = (mine[0, 0, :, lanes], other[0, :, lanes])
    k = (mine[0, 1, :, lanes], other[1, :, lanes])
    v = (mine[0, 2, :, lanes], other[2, :, lanes])
    ka = jnp.concatenate([ref[0, :, lanes] for ref in audio], axis=0)
    va = jnp.concatenate([ref[1, :, lanes] for ref in audio], axis=0)
    return q, k, v, ka, va


def scores_of(q, k, ka, scale, bias, rows):
    local = by_block(lambda kb, qb: dot(kb, qb, 1, 1), k, q) * scale
    audio = dot(ka, jnp.concatenate(q, axis=0), 1, 1) * scale
    return local, with_bias(audio, bias, rows)


def column_max(x):
    return jnp.max(x, axis=0, keepdims=True)


def column_sum(x):
    return jnp.sum(x, axis=0, keepdims=True)


def times_values(v, va, local, audio):
    return by_block(lambda vb, pb: dot(vb, pb, 0, 0), v, halves(local)) + dot(va, audio, 0, 0)


def teacher_kernel(dim, core, bias, scal, mine, other, *refs):
    *audio_refs, target = refs
    rows = audio_refs[0].shape[1]
    for i in range(target.shape[0]):
        lanes = slice(i * dim, (i + 1) * dim)
        q, k, v, ka, va = load_head(lanes, mine, other, audio_refs)
        local, audio = scores_of(q, k, ka, dim**-0.5, bias, rows)
        plain_max = column_max(local)
        plain = jnp.exp(local - plain_max)
        plain = (plain * (1.0 / column_sum(plain))).astype(jnp.bfloat16)
        highest = jnp.maximum(plain_max, column_max(audio))
        local = jnp.exp(local - highest)
        audio = jnp.exp(audio - highest)
        norm = 1.0 / (column_sum(local) + column_sum(audio))
        local = (local * norm).astype(jnp.bfloat16)
        audio = (audio * norm).astype(jnp.bfloat16)
        conditional = times_values(v, va, local, audio)
        unconditional = by_block(lambda vb, pb: dot(vb, pb, 0, 0), v, halves(plain))
        target[i] = unconditional + scal[0] * (conditional - unconditional)


def student_kernel(dim, core, bias, scal, mine, other, *refs):
    audio_refs, target = refs[:SLOTS], refs[SLOTS]
    grad_mine, grad_other, own_out, zed_out, far_out, opposite_out, totals = refs[SLOTS + 1 :]
    rows = audio_refs[0].shape[1]
    scale = dim**-0.5
    heads = target.shape[0]
    for i in range(heads):
        lanes = slice(i * dim, (i + 1) * dim)
        q, k, v, ka, va = load_head(lanes, mine, other, audio_refs)
        local, audio = scores_of(q, k, ka, scale, bias, rows)
        highest = jnp.maximum(column_max(local), column_max(audio))
        local = jnp.exp(local - highest)
        audio = jnp.exp(audio - highest)
        norm = 1.0 / (column_sum(local) + column_sum(audio))
        local = local * norm
        audio = audio * norm
        local_round = local.astype(jnp.bfloat16)
        audio_round = audio.astype(jnp.bfloat16)
        out = times_values(v, va, local_round, audio_round)
        factor = scal[2 + pl.program_id(0) * heads + i]
        residual = scal[1] * (out * factor - target[i])
        product = residual * out
        n = product.shape[1] // 2
        product = product[:, :n] + product[:, n:]
        totals[i] = jnp.sum(product.reshape(dim // 8, 8, n), axis=0)
        out_grad = (residual * factor).astype(jnp.bfloat16)
        row_delta = column_sum(out_grad.astype(jnp.float32) * out)
        grads = halves(out_grad)
        local_grad = by_block(lambda vb, gb: dot(vb, gb, 1, 0), v, grads)
        audio_grad = dot(va, out_grad, 1, 0)
        local_grad = (scale * local * (local_grad - row_delta)).astype(jnp.bfloat16)
        audio_grad = (scale * audio * (audio_grad - row_delta)).astype(jnp.bfloat16)
        query_grad = times_values(k, ka, local_grad, audio_grad).T.astype(jnp.bfloat16)
        vb = query_grad.shape[0] // 2
        score_halves = halves(local_grad)
        prob_halves = halves(local_round)
        for b, (ref, first) in enumerate(((grad_mine, (0,)), (grad_other, ()))):
            ref[(*first, 0, slice(None), lanes)] = query_grad[b * vb : (b + 1) * vb]
            key_grad = dot(score_halves[b], q[b], 1, 0)
            ref[(*first, 1, slice(None), lanes)] = key_grad.astype(jnp.bfloat16)
            value_grad = dot(prob_halves[b], grads[b], 1, 1)
            ref[(*first, 2, slice(None), lanes)] = value_grad.astype(jnp.bfloat16)
        audio_keys = dot(audio_grad, jnp.concatenate(q, axis=0), 1, 0)
        audio_values = dot(audio_round, out_grad, 1, 1)
        places = [(own_out, 0), (own_out, 1), (zed_out, 0), (zed_out, 1)]
        places += [(far_out, 0), (far_out, 1), (far_out, 2), (opposite_out, 0)]
        for slot, (ref, b) in enumerate(places):
            at = slice(slot * rows, (slot + 1) * rows)
            ref[b, 0, :, lanes] = audio_keys[at].astype(ref.dtype)
            ref[b, 1, :, lanes] = audio_values[at].astype(ref.dtype)


def specs(steps, width, vb, audio, which):
    smem = pl.BlockSpec(memory_space=pltpu.SMEM)
    mine = pl.BlockSpec((1, 3, vb, width), lambda h, c: (0, 0, 0, c[0] * steps + h))
    video = pl.BlockSpec((3, vb, width), lambda h, c: (0, 0, h))

    def piece(x):
        at = which if x.shape[0] > 2 else 0
        return pl.BlockSpec((2, x.shape[1], width), lambda h, c: (at, 0, h))

    return [smem, smem, mine, video] + [piece(x) for x in audio]


def teacher_call(core, bias, scal, mine, other, audio, head_dim):
    vb, half_width = mine.shape[2], other.shape[2]
    width = STEP_HEADS * head_dim
    steps = half_width // width
    heads = half_width // head_dim
    return pl.pallas_call(
        functools.partial(teacher_kernel, head_dim),
        grid_spec=pltpu.PrefetchScalarGridSpec(
            num_scalar_prefetch=1,
            grid=(steps,),
            in_specs=specs(steps, width, vb, audio, 0),
            out_specs=pl.BlockSpec((STEP_HEADS, head_dim, 2 * vb), lambda h, c: (h, 0, 0)),
        ),
        out_shape=jax.ShapeDtypeStruct((heads, head_dim, 2 * vb), jnp.float32),
        compiler_params=pltpu.CompilerParams(vmem_limit_bytes=VMEM),
        cost_estimate=pl.CostEstimate(
            flops=600_000_000, bytes_accessed=4_000_000, transcendentals=900_000
        ),
        name="teacher",
    )(core, bias, scal, mine, other, *audio)


def student_call(core, bias, scal, mine, other, audio, target, head_dim):
    vb, half_width = mine.shape[2], other.shape[2]
    rows = audio[0].shape[1]
    width = STEP_HEADS * head_dim
    steps = half_width // width
    in_specs = specs(steps, width, vb, audio, 1)
    heads = half_width // head_dim

    def blocks(n, dtype):
        shape = jax.ShapeDtypeStruct((n, 2, rows, half_width), dtype)
        return shape, pl.BlockSpec((n, 2, rows, width), lambda h, c: (0, 0, 0, h))

    outs = [
        (jax.ShapeDtypeStruct(mine.shape, jnp.bfloat16), in_specs[2]),
        (jax.ShapeDtypeStruct(other.shape, jnp.bfloat16), in_specs[3]),
        blocks(2, jnp.float32),
        blocks(2, jnp.float32),
        blocks(3, jnp.bfloat16),
        blocks(1, jnp.bfloat16),
        (
            jax.ShapeDtypeStruct((heads, 8, vb), jnp.float32),
            pl.BlockSpec((STEP_HEADS, 8, vb), lambda h, c: (h, 0, 0)),
        ),
    ]
    return pl.pallas_call(
        functools.partial(student_kernel, head_dim),
        grid_spec=pltpu.PrefetchScalarGridSpec(
            num_scalar_prefetch=1,
            grid=(steps,),
            in_specs=in_specs
            + [pl.BlockSpec((STEP_HEADS, head_dim, 2 * vb), lambda h, c: (h, 0, 0))],
            out_specs=[spec for _, spec in outs],
        ),
        out_shape=[shape for shape, _ in outs],
        compiler_params=pltpu.CompilerParams(vmem_limit_bytes=VMEM),
        cost_estimate=pl.CostEstimate(
            flops=900_000_000, bytes_accessed=8_000_000, transcendentals=600_000
        ),
        name="student",
    )(core, bias, scal, mine, other, *audio, target)


def swap(x, axis):
    return lax.ppermute(x, axis, [(0, 1), (1, 0)])


def everywhere(x, axes):
    n = lax.axis_size(axes)
    copies = jnp.broadcast_to(x[None], (n,) + x.shape)
    return jnp.sum(lax.all_to_all(copies, axes, 0, 0), axis=0)


def body(
    teacher_video,
    student_video,
    teacher_audio,
    student_audio,
    alignment,
    guidance_index,
    step_index,
    null_flag,
    gamma,
):
    heads = gamma.shape[1]
    width = teacher_video.shape[3]
    half_width = width // 2
    head_dim = width // heads
    half_heads = heads // 2
    tokens = teacher_video.shape[2]
    core = lax.axis_index(CORE)
    half = lax.axis_index(HALF)
    position = lax.axis_index(SEQ)
    base = position - core

    group = lax.axis_size(HALF) * lax.axis_size(CORE)
    count = lax.axis_size(SEQ)
    places = range(count)

    def inside(pairs):
        return [(a, b) for a, b in pairs if 0 <= b < count]

    far_out = inside((i, i - group if (i // 2) % 2 else i + group) for i in places)
    far_back = [(b, a) for a, b in far_out]

    def part(x, which):
        return lax.dynamic_slice_in_dim(x, which * half_width, half_width, x.ndim - 1)

    audio = jnp.concatenate([teacher_audio[0], student_audio[0]], axis=0)
    kept = part(audio, core)
    got = swap(part(audio, 1 - core), CORE)
    inner = core == half
    zed_kept, got, teacher_video, alignment, guidance_index, step_index = (
        lax.optimization_barrier(
            (swap(kept, HALF), got, teacher_video, alignment, guidance_index, step_index)
        )
    )
    zed_got, far_kept, same, opposite, teach_other, spans = lax.optimization_barrier(
        (
            swap(got, HALF),
            lax.ppermute(zed_kept, SEQ, far_out),
            lax.ppermute(jnp.where(inner, got, kept), SEQ, far_out),
            lax.ppermute(jnp.where(inner, kept, got), SEQ, far_back),
            swap(part(teacher_video[0], 1 - core), CORE),
            lax.all_gather(alignment[0, 0], CORE),
        )
    )
    far_got = [lax.ppermute(zed_got[i : i + 2], SEQ, far_out) for i in (0, 2)]
    far_got[0], student_video = lax.optimization_barrier((far_got[0], student_video))
    pupil_other = swap(part(student_video[0], 1 - core), CORE)

    side = 2 - 4 * half
    near = 7 * half
    owners = jnp.stack(
        [
            base + core,
            base + 1 - core,
            base + side + core,
            base + side + 1 - core,
            base - side + core,
            base - side + 1 - core,
            base - 3 + near,
            base + 4 - near,
        ]
    )
    span = jnp.where(core == 0, spans, spans[::-1])
    first, length = span[None, :, 0], span[None, :, 1]
    used = (owners[:, None] >= first) & (owners[:, None] < first + length) & (null_flag[0] == 0)
    bias = jnp.where(used, 0.0, -jnp.inf).astype(jnp.float32).reshape(2 * SLOTS)

    level_index = guidance_index[0]
    levels = jnp.arange(gamma.shape[0], dtype=jnp.int32)
    weight = 1.0 + 0.75 * level_index.astype(jnp.float32)
    loss_weight = 1.0 / (1.0 + step_index[0].astype(jnp.float32) / 250.0)
    factor = jnp.sum(
        jnp.where(levels[:, None] == level_index, gamma, jnp.zeros_like(gamma)), axis=0
    )
    factor = lax.dynamic_slice_in_dim(factor, core * half_heads, half_heads)
    scal = jnp.concatenate([jnp.stack([weight, loss_weight]), factor])
    which = core.astype(jnp.int32)[None]

    windows = [
        (kept, got, zed_kept, zed_got, far_kept, far_got[i], same, opposite)
        for i in range(2)
    ]
    target = teacher_call(which, bias, scal, teacher_video, teach_other, windows[0], head_dim)
    grad_video, grad_other, own, zed, far, opposite, totals = student_call(
        which, bias, scal, student_video, pupil_other, windows[1], target, head_dim
    )

    sums = jnp.sum(totals, axis=(1, 2))
    head_totals = lax.dynamic_update_slice_in_dim(
        jnp.zeros((heads,), jnp.float32), sums, core * half_heads, 0
    )
    contribution = jnp.where(
        levels[:, None] == level_index, head_totals[None, :], jnp.zeros_like(gamma)
    )
    far_in = lax.ppermute(far, SEQ, far_back)
    far_in, contribution = lax.optimization_barrier((far_in, everywhere(contribution, FIRST)))
    far_in = far_in.astype(jnp.float32)
    opposite_in = lax.ppermute(opposite[0], SEQ, far_out).astype(jnp.float32)
    zed_in = swap((zed + far_in[:2]).astype(jnp.bfloat16), HALF)
    zed_in, gamma_grad = lax.optimization_barrier((zed_in, everywhere(contribution, SECOND)))
    zed_in = zed_in.astype(jnp.float32)
    near_in = (far_in[2], opposite_in)
    keep = own[0] + jnp.where(inner, near_in[1], near_in[0])
    leave = own[1] + jnp.where(inner, near_in[0], near_in[1])
    keep = (keep + zed_in[0]).astype(jnp.bfloat16)
    arrived = swap((leave + zed_in[1]).astype(jnp.bfloat16), CORE)
    gamma_grad, arrived = lax.optimization_barrier((lax.psum(gamma_grad, CORE), arrived))
    grad_audio = jnp.where(
        core == 0,
        jnp.concatenate([keep, arrived], axis=-1),
        jnp.concatenate([arrived, keep], axis=-1),
    )[None]
    grad_video = lax.dynamic_update_slice_in_dim(
        grad_video, swap(grad_other, CORE)[None], (1 - core) * half_width, 3
    )

    gamma_grad = gamma_grad / (tokens * count * head_dim)
    return (grad_video, grad_audio, gamma_grad)


def solution(mesh):
    finer = Mesh(
        mesh.devices.reshape(8, 4, 2, 2, mesh.shape["dp"]),
        ("seq_0", "seq_1", "seq_2", "seq_3", "dp"),
    )
    in_specs = (
        P("dp", None, SEQ, None),
        P("dp", None, SEQ, None),
        P("dp", None, SEQ, None),
        P("dp", None, SEQ, None),
        P("dp", SEQ, None),
        P("dp"),
        P("dp"),
        P("dp"),
        P(),
    )
    out_specs = (P("dp", None, SEQ, None), P("dp", None, SEQ, None), P())
    return jax.shard_map(body, mesh=finer, in_specs=in_specs, out_specs=out_specs, check_vma=False)
```

```python
import functools

import jax
import jax.numpy as jnp
from jax import lax
from jax.experimental import pallas as pl
from jax.experimental.pallas import tpu as pltpu
from jax.sharding import Mesh
from jax.sharding import PartitionSpec as P

SEQ = ("seq_0", "seq_1", "seq_2", "seq_3")
PLANE = ("seq_0", "seq_1")
COLUMN = ("seq_2", "seq_3", "dp")
HALF = "seq_2"
CORE = "seq_3"
SLOTS = 8
STEP_HEADS = 6
VMEM = 36 * 1024 * 1024


def dot(a, b, contract_a, contract_b):
    return lax.dot_general(
        a, b, (((contract_a,), (contract_b,)), ((), ())), preferred_element_type=jnp.float32
    )


def by_block(f, *pairs):
    return jnp.concatenate([f(*args) for args in zip(*pairs)], axis=1)


def halves(x):
    n = x.shape[1] // 2
    return x[:, :n], x[:, n:]


def with_bias(scores, bias, rows):
    out = []
    for slot in range(SLOTS):
        piece = halves(scores[slot * rows : (slot + 1) * rows])
        out.append(jnp.concatenate([piece[b] + bias[2 * slot + b] for b in range(2)], axis=1))
    return jnp.concatenate(out, axis=0)


def load_head(lanes, mine, other, audio):
    q = (mine[0, 0, :, lanes], other[0, :, lanes])
    k = (mine[0, 1, :, lanes], other[1, :, lanes])
    v = (mine[0, 2, :, lanes], other[2, :, lanes])
    own, zed, far, same, opposite = audio

    def window(i):
        pieces = [ref[b, i, :, lanes] for ref in (own, zed, far) for b in range(2)]
        return jnp.concatenate(pieces + [same[i, :, lanes], opposite[i, :, lanes]], axis=0)

    return q, k, v, window(0), window(1)


def scores_of(q, k, ka, scale, bias, rows):
    local = by_block(lambda kb, qb: dot(kb, qb, 1, 1), k, q) * scale
    audio = dot(ka, jnp.concatenate(q, axis=0), 1, 1) * scale
    return local, with_bias(audio, bias, rows)


def column_max(x):
    return jnp.max(x, axis=0, keepdims=True)


def column_sum(x):
    return jnp.sum(x, axis=0, keepdims=True)


def times_values(v, va, local, audio):
    return by_block(lambda vb, pb: dot(vb, pb, 0, 0), v, halves(local)) + dot(va, audio, 0, 0)


def teacher_kernel(dim, core, bias, scal, mine, other, *refs):
    *audio_refs, target = refs
    rows = audio_refs[0].shape[2]
    for i in range(target.shape[0]):
        lanes = slice(i * dim, (i + 1) * dim)
        q, k, v, ka, va = load_head(lanes, mine, other, audio_refs)
        local, audio = scores_of(q, k, ka, dim**-0.5, bias, rows)
        plain_max = column_max(local)
        plain = jnp.exp(local - plain_max)
        plain = (plain * (1.0 / column_sum(plain))).astype(jnp.bfloat16)
        highest = jnp.maximum(plain_max, column_max(audio))
        local = jnp.exp(local - highest)
        audio = jnp.exp(audio - highest)
        norm = 1.0 / (column_sum(local) + column_sum(audio))
        local = (local * norm).astype(jnp.bfloat16)
        audio = (audio * norm).astype(jnp.bfloat16)
        conditional = times_values(v, va, local, audio)
        unconditional = by_block(lambda vb, pb: dot(vb, pb, 0, 0), v, halves(plain))
        target[i] = unconditional + scal[0] * (conditional - unconditional)


def student_kernel(dim, core, bias, scal, mine, other, *refs):
    audio_refs, target = refs[:5], refs[5]
    grad_mine, grad_other, own_out, zed_out, far_out, opposite_out, totals = refs[6:]
    rows = audio_refs[0].shape[2]
    scale = dim**-0.5
    heads = target.shape[0]
    for i in range(heads):
        lanes = slice(i * dim, (i + 1) * dim)
        q, k, v, ka, va = load_head(lanes, mine, other, audio_refs)
        local, audio = scores_of(q, k, ka, scale, bias, rows)
        highest = jnp.maximum(column_max(local), column_max(audio))
        local = jnp.exp(local - highest)
        audio = jnp.exp(audio - highest)
        norm = 1.0 / (column_sum(local) + column_sum(audio))
        local = local * norm
        audio = audio * norm
        local_round = local.astype(jnp.bfloat16)
        audio_round = audio.astype(jnp.bfloat16)
        out = times_values(v, va, local_round, audio_round)
        factor = scal[2 + pl.program_id(0) * heads + i]
        residual = scal[1] * (out * factor - target[i])
        product = residual * out
        n = product.shape[1] // 2
        product = product[:, :n] + product[:, n:]
        totals[i] = jnp.sum(product.reshape(dim // 8, 8, n), axis=0)
        out_grad = (residual * factor).astype(jnp.bfloat16)
        row_delta = column_sum(out_grad.astype(jnp.float32) * out)
        grads = halves(out_grad)
        local_grad = by_block(lambda vb, gb: dot(vb, gb, 1, 0), v, grads)
        audio_grad = dot(va, out_grad, 1, 0)
        local_grad = (scale * local * (local_grad - row_delta)).astype(jnp.bfloat16)
        audio_grad = (scale * audio * (audio_grad - row_delta)).astype(jnp.bfloat16)
        query_grad = times_values(k, ka, local_grad, audio_grad).T.astype(jnp.bfloat16)
        vb = query_grad.shape[0] // 2
        score_halves = halves(local_grad)
        prob_halves = halves(local_round)
        for b, (ref, first) in enumerate(((grad_mine, (0,)), (grad_other, ()))):
            ref[(*first, 0, slice(None), lanes)] = query_grad[b * vb : (b + 1) * vb]
            key_grad = dot(score_halves[b], q[b], 1, 0)
            ref[(*first, 1, slice(None), lanes)] = key_grad.astype(jnp.bfloat16)
            value_grad = dot(prob_halves[b], grads[b], 1, 1)
            ref[(*first, 2, slice(None), lanes)] = value_grad.astype(jnp.bfloat16)
        audio_keys = dot(audio_grad, jnp.concatenate(q, axis=0), 1, 0)
        audio_values = dot(audio_round, out_grad, 1, 1)
        places = [(own_out, 0), (own_out, 1), (zed_out, 0), (zed_out, 1)]
        places += [(far_out, 0), (far_out, 1), (far_out, 2), (opposite_out, 0)]
        for slot, (ref, b) in enumerate(places):
            at = slice(slot * rows, (slot + 1) * rows)
            ref[b, 0, :, lanes] = audio_keys[at].astype(ref.dtype)
            ref[b, 1, :, lanes] = audio_values[at].astype(ref.dtype)


def specs(steps, width, vb, audio, which):
    smem = pl.BlockSpec(memory_space=pltpu.SMEM)
    mine = pl.BlockSpec((1, 3, vb, width), lambda h, c: (0, 0, 0, c[0] * steps + h))
    video = pl.BlockSpec((3, vb, width), lambda h, c: (0, 0, h))

    rows = audio[0].shape[2]
    pair = pl.BlockSpec((2, 2, rows, width), lambda h, c: (0, 0, 0, h))
    single = pl.BlockSpec((2, rows, width), lambda h, c: (which, 0, h))
    return [smem, smem, mine, video] + [pair] * 3 + [single] * 2


def teacher_call(core, bias, scal, mine, other, audio, head_dim):
    vb, half_width = mine.shape[2], other.shape[2]
    width = STEP_HEADS * head_dim
    steps = half_width // width
    heads = half_width // head_dim
    return pl.pallas_call(
        functools.partial(teacher_kernel, head_dim),
        grid_spec=pltpu.PrefetchScalarGridSpec(
            num_scalar_prefetch=1,
            grid=(steps,),
            in_specs=specs(steps, width, vb, audio, 0),
            out_specs=pl.BlockSpec((STEP_HEADS, head_dim, 2 * vb), lambda h, c: (h, 0, 0)),
        ),
        out_shape=jax.ShapeDtypeStruct((heads, head_dim, 2 * vb), jnp.float32),
        compiler_params=pltpu.CompilerParams(vmem_limit_bytes=VMEM),
        cost_estimate=pl.CostEstimate(
            flops=600_000_000, bytes_accessed=4_000_000, transcendentals=900_000
        ),
        name="teacher",
    )(core, bias, scal, mine, other, *audio)


def student_call(core, bias, scal, mine, other, audio, target, head_dim):
    vb, half_width = mine.shape[2], other.shape[2]
    rows = audio[0].shape[2]
    width = STEP_HEADS * head_dim
    steps = half_width // width
    in_specs = specs(steps, width, vb, audio, 1)
    heads = half_width // head_dim

    def blocks(n, dtype):
        shape = jax.ShapeDtypeStruct((n, 2, rows, half_width), dtype)
        return shape, pl.BlockSpec((n, 2, rows, width), lambda h, c: (0, 0, 0, h))

    outs = [
        (jax.ShapeDtypeStruct(mine.shape, jnp.bfloat16), in_specs[2]),
        (
            jax.ShapeDtypeStruct((3, vb, half_width), jnp.bfloat16),
            pl.BlockSpec((3, vb, width), lambda h, c: (0, 0, h)),
        ),
        blocks(2, jnp.float32),
        blocks(2, jnp.float32),
        blocks(3, jnp.bfloat16),
        blocks(1, jnp.bfloat16),
        (
            jax.ShapeDtypeStruct((heads, 8, vb), jnp.float32),
            pl.BlockSpec((STEP_HEADS, 8, vb), lambda h, c: (h, 0, 0)),
        ),
    ]
    return pl.pallas_call(
        functools.partial(student_kernel, head_dim),
        grid_spec=pltpu.PrefetchScalarGridSpec(
            num_scalar_prefetch=1,
            grid=(steps,),
            in_specs=in_specs
            + [pl.BlockSpec((STEP_HEADS, head_dim, 2 * vb), lambda h, c: (h, 0, 0))],
            out_specs=[spec for _, spec in outs],
        ),
        out_shape=[shape for shape, _ in outs],
        compiler_params=pltpu.CompilerParams(vmem_limit_bytes=VMEM),
        cost_estimate=pl.CostEstimate(
            flops=900_000_000, bytes_accessed=8_000_000, transcendentals=600_000
        ),
        name="student",
    )(core, bias, scal, mine, other, *audio, target)


def swap(x, axis):
    return lax.ppermute(x, axis, [(0, 1), (1, 0)])


def everywhere(x, axes):
    n = lax.axis_size(axes)
    copies = jnp.broadcast_to(x[None], (n,) + x.shape)
    return jnp.sum(lax.all_to_all(copies, axes, 0, 0), axis=0)


def body(
    teacher_video,
    student_video,
    teacher_audio,
    student_audio,
    alignment,
    guidance_index,
    step_index,
    null_flag,
    gamma,
):
    heads = gamma.shape[1]
    width = teacher_video.shape[3]
    half_width = width // 2
    head_dim = width // heads
    half_heads = heads // 2
    tokens = teacher_video.shape[2]
    core = lax.axis_index(CORE)
    half = lax.axis_index(HALF)
    position = lax.axis_index(SEQ)
    base = position - core

    group = lax.axis_size(HALF) * lax.axis_size(CORE)
    count = lax.axis_size(SEQ)
    places = range(count)

    def inside(pairs):
        return [(a, b) for a, b in pairs if 0 <= b < count]

    far_out = inside((i, i - group if (i // 2) % 2 else i + group) for i in places)
    far_back = [(b, a) for a, b in far_out]

    def part(x, which):
        return lax.dynamic_slice_in_dim(x, which * half_width, half_width, x.ndim - 1)

    span = alignment[0, 0]
    rows = teacher_audio.shape[2]
    upper = lax.broadcasted_iota(jnp.int32, (1, rows, half_width), 1) < rows // 2
    slab = jnp.where(upper, span[0], span[1]).astype(jnp.bfloat16)
    audio = jnp.concatenate([teacher_audio[0], student_audio[0]], axis=0)
    kept = part(audio, core)
    received = swap(jnp.concatenate([part(audio, 1 - core), slab], axis=0), CORE)
    got = received[:4]
    span_other = jnp.stack([received[4, 0, 0], received[4, rows // 2, 0]]).astype(jnp.int32)
    inner = core == half
    pairs = [jnp.stack([kept[i : i + 2], got[i : i + 2]]) for i in (0, 2)]
    zeds = [swap(pair, HALF) for pair in pairs]
    zeds[0], teacher_video, student_video, guidance_index, step_index, span_other = (
        lax.optimization_barrier(
            (zeds[0], teacher_video, student_video, guidance_index, step_index, span_other)
        )
    )
    teach_other = swap(part(teacher_video[0], 1 - core), CORE)
    pupil_other = swap(part(student_video[0], 1 - core), CORE)
    same = lax.ppermute(jnp.where(inner, got, kept), SEQ, far_out)
    opposite = lax.ppermute(jnp.where(inner, kept, got), SEQ, far_back)
    zeds[1], same, opposite = lax.optimization_barrier(
        (zeds[1], same, opposite)
    )
    zeds, teach_other = lax.optimization_barrier(
        (zeds, teach_other)
    )
    fars = [lax.ppermute(zed, SEQ, far_out) for zed in zeds]

    side = 2 - 4 * half
    near = 7 * half
    owners = jnp.stack(
        [
            base + core,
            base + 1 - core,
            base + side + core,
            base + side + 1 - core,
            base - side + core,
            base - side + 1 - core,
            base - 3 + near,
            base + 4 - near,
        ]
    )
    spans = jnp.stack([span, span_other])
    first, length = spans[None, :, 0], spans[None, :, 1]
    used = (owners[:, None] >= first) & (owners[:, None] < first + length) & (null_flag[0] == 0)
    bias = jnp.where(used, 0.0, -jnp.inf).astype(jnp.float32).reshape(2 * SLOTS)

    level_index = guidance_index[0]
    levels = jnp.arange(gamma.shape[0], dtype=jnp.int32)
    weight = 1.0 + 0.75 * level_index.astype(jnp.float32)
    loss_weight = 1.0 / (1.0 + step_index[0].astype(jnp.float32) / 250.0)
    factor = jnp.sum(
        jnp.where(levels[:, None] == level_index, gamma, jnp.zeros_like(gamma)), axis=0
    )
    factor = lax.dynamic_slice_in_dim(factor, core * half_heads, half_heads)
    scal = jnp.concatenate([jnp.stack([weight, loss_weight]), factor])
    which = core.astype(jnp.int32)[None]

    windows = [(pair, zed, far, same, opposite) for pair, zed, far in zip(pairs, zeds, fars)]
    target = teacher_call(which, bias, scal, teacher_video, teach_other, windows[0], head_dim)
    grad_video, grad_other, own, zed, far, opposite, totals = student_call(
        which, bias, scal, student_video, pupil_other, windows[1], target, head_dim
    )

    sums = jnp.sum(totals, axis=(1, 2))
    head_totals = lax.dynamic_update_slice_in_dim(
        jnp.zeros((heads,), jnp.float32), sums, core * half_heads, 0
    )
    contribution = jnp.where(
        levels[:, None] == level_index, head_totals[None, :], jnp.zeros_like(gamma)
    )
    far_in = lax.ppermute(far, SEQ, far_back)
    opposite_in = lax.ppermute(opposite[0], SEQ, far_out)
    other_in = swap(grad_other, CORE)
    far_in, opposite_in, other_in, contribution = lax.optimization_barrier(
        (far_in, opposite_in, other_in, contribution)
    )
    grad_video = lax.dynamic_update_slice_in_dim(
        grad_video, other_in[None], (1 - core) * half_width, 3
    )
    far_in = far_in.astype(jnp.float32)
    zed_in = swap((zed + far_in[:2]).astype(jnp.bfloat16), HALF)
    near_in = (far_in[2], opposite_in.astype(jnp.float32))
    keep = own[0] + jnp.where(inner, near_in[1], near_in[0])
    leave = own[1] + jnp.where(inner, near_in[0], near_in[1])
    zed_in, contribution, keep, leave, grad_video = lax.optimization_barrier(
        (zed_in, everywhere(contribution, COLUMN), keep, leave, grad_video)
    )
    zed_in = zed_in.astype(jnp.float32)
    keep = (keep + zed_in[0]).astype(jnp.bfloat16)
    arrived = swap((leave + zed_in[1]).astype(jnp.bfloat16), CORE)
    gamma_grad, arrived = lax.optimization_barrier((everywhere(contribution, PLANE), arrived))
    grad_audio = jnp.where(
        core == 0,
        jnp.concatenate([keep, arrived], axis=-1),
        jnp.concatenate([arrived, keep], axis=-1),
    )[None]
    gamma_grad = gamma_grad / (tokens * count * head_dim)
    return (grad_video, grad_audio, gamma_grad)


def solution(mesh):
    finer = Mesh(
        mesh.devices.reshape(8, 4, 2, 2, mesh.shape["dp"]),
        ("seq_0", "seq_1", "seq_2", "seq_3", "dp"),
    )
    in_specs = (
        P("dp", None, SEQ, None),
        P("dp", None, SEQ, None),
        P("dp", None, SEQ, None),
        P("dp", None, SEQ, None),
        P("dp", SEQ, None),
        P("dp"),
        P("dp"),
        P("dp"),
        P(),
    )
    out_specs = (P("dp", None, SEQ, None), P("dp", None, SEQ, None), P())
    return jax.shard_map(body, mesh=finer, in_specs=in_specs, out_specs=out_specs, check_vma=False)
```

```python
import functools

import jax
import jax.numpy as jnp
from jax import lax
from jax.experimental import pallas as pl
from jax.experimental.pallas import tpu as pltpu
from jax.sharding import Mesh
from jax.sharding import PartitionSpec as P

SEQ = ("seq_0", "seq_1", "seq_2", "seq_3")
PLANE = ("seq_0", "seq_1")
COLUMN = ("seq_2", "seq_3", "dp")
HALF = "seq_2"
CORE = "seq_3"
SLOTS = 8
STEP_HEADS = 3
VMEM = 28 * 1024 * 1024


def dot(a, b, contract_a, contract_b):
    return lax.dot_general(
        a, b, (((contract_a,), (contract_b,)), ((), ())), preferred_element_type=jnp.float32
    )


def by_block(f, *pairs):
    return jnp.concatenate([f(*args) for args in zip(*pairs)], axis=1)


def halves(x):
    n = x.shape[1] // 2
    return x[:, :n], x[:, n:]


def with_bias(scores, bias, rows):
    out = []
    for slot in range(SLOTS):
        piece = halves(scores[slot * rows : (slot + 1) * rows])
        out.append(jnp.concatenate([piece[b] + bias[2 * slot + b] for b in range(2)], axis=1))
    return jnp.concatenate(out, axis=0)


def load_head(lanes, mine, other, audio):
    q = (mine[0, 0, :, lanes], other[0, :, lanes])
    k = (mine[0, 1, :, lanes], other[1, :, lanes])
    v = (mine[0, 2, :, lanes], other[2, :, lanes])
    own, zed, far, same, opposite = audio

    def window(i):
        pieces = [ref[b, i, :, lanes] for ref in (own, zed, far) for b in range(2)]
        return jnp.concatenate(pieces + [same[i, :, lanes], opposite[i, :, lanes]], axis=0)

    return q, k, v, window(0), window(1)


def scores_of(q, k, ka, scale, bias, rows):
    local = by_block(lambda kb, qb: dot(kb, qb, 1, 1), k, q) * scale
    audio = dot(ka, jnp.concatenate(q, axis=0), 1, 1) * scale
    return local, with_bias(audio, bias, rows)


def column_max(x):
    return jnp.max(x, axis=0, keepdims=True)


def column_sum(x):
    return jnp.sum(x, axis=0, keepdims=True)


def times_values(v, va, local, audio):
    return by_block(lambda vb, pb: dot(vb, pb, 0, 0), v, halves(local)) + dot(va, audio, 0, 0)


def teacher_kernel(dim, core, bias, scal, mine, other, *refs):
    *audio_refs, target = refs
    rows = audio_refs[0].shape[2]
    for i in range(target.shape[0]):
        lanes = slice(i * dim, (i + 1) * dim)
        q, k, v, ka, va = load_head(lanes, mine, other, audio_refs)
        local, audio = scores_of(q, k, ka, dim**-0.5, bias, rows)
        plain_max = column_max(local)
        plain = jnp.exp(local - plain_max)
        plain = (plain * (1.0 / column_sum(plain))).astype(jnp.bfloat16)
        highest = jnp.maximum(plain_max, column_max(audio))
        local = jnp.exp(local - highest)
        audio = jnp.exp(audio - highest)
        norm = 1.0 / (column_sum(local) + column_sum(audio))
        local = (local * norm).astype(jnp.bfloat16)
        audio = (audio * norm).astype(jnp.bfloat16)
        conditional = times_values(v, va, local, audio)
        unconditional = by_block(lambda vb, pb: dot(vb, pb, 0, 0), v, halves(plain))
        target[i] = unconditional + scal[0] * (conditional - unconditional)


def student_kernel(dim, core, bias, scal, mine, other, *refs):
    audio_refs, target = refs[:5], refs[5]
    grad_mine, grad_other, own_out, zed_out, far_out, opposite_out, totals = refs[6:]
    rows = audio_refs[0].shape[2]
    scale = dim**-0.5
    heads = target.shape[0]
    for i in range(heads):
        lanes = slice(i * dim, (i + 1) * dim)
        q, k, v, ka, va = load_head(lanes, mine, other, audio_refs)
        local, audio = scores_of(q, k, ka, scale, bias, rows)
        highest = jnp.maximum(column_max(local), column_max(audio))
        local = jnp.exp(local - highest)
        audio = jnp.exp(audio - highest)
        norm = 1.0 / (column_sum(local) + column_sum(audio))
        local = local * norm
        audio = audio * norm
        local_round = local.astype(jnp.bfloat16)
        audio_round = audio.astype(jnp.bfloat16)
        out = times_values(v, va, local_round, audio_round)
        factor = scal[2 + pl.program_id(0) * heads + i]
        residual = scal[1] * (out * factor - target[i])
        product = residual * out
        n = product.shape[1] // 2
        product = product[:, :n] + product[:, n:]
        totals[i] = jnp.sum(product.reshape(dim // 8, 8, n), axis=0)
        out_grad = (residual * factor).astype(jnp.bfloat16)
        row_delta = column_sum(out_grad.astype(jnp.float32) * out)
        grads = halves(out_grad)
        local_grad = by_block(lambda vb, gb: dot(vb, gb, 1, 0), v, grads)
        audio_grad = dot(va, out_grad, 1, 0)
        local_grad = (scale * local * (local_grad - row_delta)).astype(jnp.bfloat16)
        audio_grad = (scale * audio * (audio_grad - row_delta)).astype(jnp.bfloat16)
        query_grad = times_values(k, ka, local_grad, audio_grad).T.astype(jnp.bfloat16)
        vb = query_grad.shape[0] // 2
        score_halves = halves(local_grad)
        prob_halves = halves(local_round)
        for b, (ref, first) in enumerate(((grad_mine, (0,)), (grad_other, ()))):
            ref[(*first, 0, slice(None), lanes)] = query_grad[b * vb : (b + 1) * vb]
            key_grad = dot(score_halves[b], q[b], 1, 0)
            ref[(*first, 1, slice(None), lanes)] = key_grad.astype(jnp.bfloat16)
            value_grad = dot(prob_halves[b], grads[b], 1, 1)
            ref[(*first, 2, slice(None), lanes)] = value_grad.astype(jnp.bfloat16)
        audio_keys = dot(audio_grad, jnp.concatenate(q, axis=0), 1, 0)
        audio_values = dot(audio_round, out_grad, 1, 1)
        places = [(own_out, 0), (own_out, 1), (zed_out, 0), (zed_out, 1)]
        places += [(far_out, 0), (far_out, 1), (far_out, 2), (opposite_out, 0)]
        for slot, (ref, b) in enumerate(places):
            at = slice(slot * rows, (slot + 1) * rows)
            ref[b, 0, :, lanes] = audio_keys[at].astype(ref.dtype)
            ref[b, 1, :, lanes] = audio_values[at].astype(ref.dtype)


def specs(steps, width, vb, audio, which):
    smem = pl.BlockSpec(memory_space=pltpu.SMEM)
    mine = pl.BlockSpec((1, 3, vb, width), lambda h, c: (0, 0, 0, c[0] * steps + h))
    video = pl.BlockSpec((3, vb, width), lambda h, c: (0, 0, h))

    rows = audio[0].shape[2]
    pair = pl.BlockSpec((2, 2, rows, width), lambda h, c: (0, 0, 0, h))
    single = pl.BlockSpec((2, rows, width), lambda h, c: (which, 0, h))
    return [smem, smem, mine, video] + [pair] * 3 + [single] * 2


def teacher_call(core, bias, scal, mine, other, audio, head_dim):
    vb, half_width = mine.shape[2], other.shape[2]
    width = STEP_HEADS * head_dim
    steps = half_width // width
    heads = half_width // head_dim
    return pl.pallas_call(
        functools.partial(teacher_kernel, head_dim),
        grid_spec=pltpu.PrefetchScalarGridSpec(
            num_scalar_prefetch=1,
            grid=(steps,),
            in_specs=specs(steps, width, vb, audio, 0),
            out_specs=pl.BlockSpec((STEP_HEADS, head_dim, 2 * vb), lambda h, c: (h, 0, 0)),
        ),
        out_shape=jax.ShapeDtypeStruct((heads, head_dim, 2 * vb), jnp.float32),
        compiler_params=pltpu.CompilerParams(vmem_limit_bytes=VMEM),
        cost_estimate=pl.CostEstimate(
            flops=600_000_000, bytes_accessed=4_000_000, transcendentals=900_000
        ),
        name="teacher",
    )(core, bias, scal, mine, other, *audio)


def student_call(core, bias, scal, mine, other, audio, target, head_dim):
    vb, half_width = mine.shape[2], other.shape[2]
    rows = audio[0].shape[2]
    width = STEP_HEADS * head_dim
    steps = half_width // width
    in_specs = specs(steps, width, vb, audio, 1)
    heads = half_width // head_dim

    def blocks(n, dtype):
        shape = jax.ShapeDtypeStruct((n, 2, rows, half_width), dtype)
        return shape, pl.BlockSpec((n, 2, rows, width), lambda h, c: (0, 0, 0, h))

    outs = [
        (jax.ShapeDtypeStruct(mine.shape, jnp.bfloat16), in_specs[2]),
        (jax.ShapeDtypeStruct(other.shape, jnp.bfloat16), in_specs[3]),
        blocks(2, jnp.float32),
        blocks(2, jnp.float32),
        blocks(3, jnp.bfloat16),
        blocks(1, jnp.bfloat16),
        (
            jax.ShapeDtypeStruct((heads, 8, vb), jnp.float32),
            pl.BlockSpec((STEP_HEADS, 8, vb), lambda h, c: (h, 0, 0)),
        ),
    ]
    return pl.pallas_call(
        functools.partial(student_kernel, head_dim),
        grid_spec=pltpu.PrefetchScalarGridSpec(
            num_scalar_prefetch=1,
            grid=(steps,),
            in_specs=in_specs
            + [pl.BlockSpec((STEP_HEADS, head_dim, 2 * vb), lambda h, c: (h, 0, 0))],
            out_specs=[spec for _, spec in outs],
        ),
        out_shape=[shape for shape, _ in outs],
        compiler_params=pltpu.CompilerParams(vmem_limit_bytes=VMEM),
        cost_estimate=pl.CostEstimate(
            flops=900_000_000, bytes_accessed=8_000_000, transcendentals=600_000
        ),
        name="student",
    )(core, bias, scal, mine, other, *audio, target)


def swap(x, axis):
    return lax.ppermute(x, axis, [(0, 1), (1, 0)])


def everywhere(x, axes):
    n = lax.axis_size(axes)
    copies = jnp.broadcast_to(x[None], (n,) + x.shape)
    return jnp.sum(lax.all_to_all(copies, axes, 0, 0), axis=0)


def body(
    teacher_video,
    student_video,
    teacher_audio,
    student_audio,
    alignment,
    guidance_index,
    step_index,
    null_flag,
    gamma,
):
    heads = gamma.shape[1]
    width = teacher_video.shape[3]
    half_width = width // 2
    head_dim = width // heads
    half_heads = heads // 2
    tokens = teacher_video.shape[2]
    core = lax.axis_index(CORE)
    half = lax.axis_index(HALF)
    position = lax.axis_index(SEQ)
    base = position - core

    group = lax.axis_size(HALF) * lax.axis_size(CORE)
    count = lax.axis_size(SEQ)
    places = range(count)

    def inside(pairs):
        return [(a, b) for a, b in pairs if 0 <= b < count]

    far_out = inside((i, i - group if (i // 2) % 2 else i + group) for i in places)
    far_back = [(b, a) for a, b in far_out]

    def part(x, which):
        return lax.dynamic_slice_in_dim(x, which * half_width, half_width, x.ndim - 1)

    audio = jnp.concatenate([teacher_audio[0], student_audio[0]], axis=0)
    kept = part(audio, core)
    got = swap(part(audio, 1 - core), CORE)
    inner = core == half
    pairs = [jnp.stack([kept[i : i + 2], got[i : i + 2]]) for i in (0, 2)]
    zeds = [swap(pair, HALF) for pair in pairs]
    zeds[0], teacher_video, student_video, alignment, guidance_index, step_index = (
        lax.optimization_barrier(
            (zeds[0], teacher_video, student_video, alignment, guidance_index, step_index)
        )
    )
    same = lax.ppermute(jnp.where(inner, got, kept), SEQ, far_out)
    opposite = lax.ppermute(jnp.where(inner, kept, got), SEQ, far_back)
    fars = [lax.ppermute(zed, SEQ, far_out) for zed in zeds]
    teach_other = swap(part(teacher_video[0], 1 - core), CORE)
    pupil_other = swap(part(student_video[0], 1 - core), CORE)
    spans = lax.all_gather(alignment[0, 0], CORE)

    side = 2 - 4 * half
    near = 7 * half
    owners = jnp.stack(
        [
            base + core,
            base + 1 - core,
            base + side + core,
            base + side + 1 - core,
            base - side + core,
            base - side + 1 - core,
            base - 3 + near,
            base + 4 - near,
        ]
    )
    span = jnp.where(core == 0, spans, spans[::-1])
    first, length = span[None, :, 0], span[None, :, 1]
    used = (owners[:, None] >= first) & (owners[:, None] < first + length) & (null_flag[0] == 0)
    bias = jnp.where(used, 0.0, -jnp.inf).astype(jnp.float32).reshape(2 * SLOTS)

    level_index = guidance_index[0]
    levels = jnp.arange(gamma.shape[0], dtype=jnp.int32)
    weight = 1.0 + 0.75 * level_index.astype(jnp.float32)
    loss_weight = 1.0 / (1.0 + step_index[0].astype(jnp.float32) / 250.0)
    factor = jnp.sum(
        jnp.where(levels[:, None] == level_index, gamma, jnp.zeros_like(gamma)), axis=0
    )
    factor = lax.dynamic_slice_in_dim(factor, core * half_heads, half_heads)
    scal = jnp.concatenate([jnp.stack([weight, loss_weight]), factor])
    which = core.astype(jnp.int32)[None]

    windows = [(pair, zed, far, same, opposite) for pair, zed, far in zip(pairs, zeds, fars)]
    target = teacher_call(which, bias, scal, teacher_video, teach_other, windows[0], head_dim)
    grad_video, grad_other, own, zed, far, opposite, totals = student_call(
        which, bias, scal, student_video, pupil_other, windows[1], target, head_dim
    )

    sums = jnp.sum(totals, axis=(1, 2))
    head_totals = lax.dynamic_update_slice_in_dim(
        jnp.zeros((heads,), jnp.float32), sums, core * half_heads, 0
    )
    contribution = jnp.where(
        levels[:, None] == level_index, head_totals[None, :], jnp.zeros_like(gamma)
    )
    far_in = lax.ppermute(far, SEQ, far_back)
    far_in, contribution = lax.optimization_barrier((far_in, everywhere(contribution, COLUMN)))
    far_in = far_in.astype(jnp.float32)
    opposite_in = lax.ppermute(opposite[0], SEQ, far_out).astype(jnp.float32)
    zed_in = swap((zed + far_in[:2]).astype(jnp.bfloat16), HALF)
    zed_in, gamma_grad = lax.optimization_barrier((zed_in, everywhere(contribution, PLANE)))
    zed_in = zed_in.astype(jnp.float32)
    near_in = (far_in[2], opposite_in)
    keep = own[0] + jnp.where(inner, near_in[1], near_in[0])
    leave = own[1] + jnp.where(inner, near_in[0], near_in[1])
    keep = (keep + zed_in[0]).astype(jnp.bfloat16)
    arrived = swap((leave + zed_in[1]).astype(jnp.bfloat16), CORE)
    grad_audio = jnp.where(
        core == 0,
        jnp.concatenate([keep, arrived], axis=-1),
        jnp.concatenate([arrived, keep], axis=-1),
    )[None]
    grad_video = lax.dynamic_update_slice_in_dim(
        grad_video, swap(grad_other, CORE)[None], (1 - core) * half_width, 3
    )

    gamma_grad = gamma_grad / (tokens * count * head_dim)
    return (grad_video, grad_audio, gamma_grad)


def solution(mesh):
    finer = Mesh(
        mesh.devices.reshape(8, 4, 2, 2, mesh.shape["dp"]),
        ("seq_0", "seq_1", "seq_2", "seq_3", "dp"),
    )
    in_specs = (
        P("dp", None, SEQ, None),
        P("dp", None, SEQ, None),
        P("dp", None, SEQ, None),
        P("dp", None, SEQ, None),
        P("dp", SEQ, None),
        P("dp"),
        P("dp"),
        P("dp"),
        P(),
    )
    out_specs = (P("dp", None, SEQ, None), P("dp", None, SEQ, None), P())
    return jax.shard_map(body, mesh=finer, in_specs=in_specs, out_specs=out_specs, check_vma=False)
```

```python
import functools

import jax
import jax.numpy as jnp
from jax import lax
from jax.experimental import pallas as pl
from jax.experimental.pallas import tpu as pltpu
from jax.sharding import Mesh
from jax.sharding import PartitionSpec as P

SEQ = ("seq_0", "seq_1", "seq_2", "seq_3")
PLANE = ("seq_0", "seq_1")
COLUMN = ("seq_2", "seq_3", "dp")
HALF = "seq_2"
CORE = "seq_3"
SLOTS = 8
STEP_HEADS = 3
VMEM = 28 * 1024 * 1024


def dot(a, b, contract_a, contract_b):
    return lax.dot_general(
        a, b, (((contract_a,), (contract_b,)), ((), ())), preferred_element_type=jnp.float32
    )


def by_block(f, *pairs):
    return jnp.concatenate([f(*args) for args in zip(*pairs)], axis=1)


def halves(x):
    n = x.shape[1] // 2
    return x[:, :n], x[:, n:]


def with_bias(scores, bias, rows):
    out = []
    for slot in range(SLOTS):
        piece = halves(scores[slot * rows : (slot + 1) * rows])
        out.append(jnp.concatenate([piece[b] + bias[2 * slot + b] for b in range(2)], axis=1))
    return jnp.concatenate(out, axis=0)


def load_head(lanes, mine, other, audio):
    q = (mine[0, 0, :, lanes], other[0, :, lanes])
    k = (mine[0, 1, :, lanes], other[1, :, lanes])
    v = (mine[0, 2, :, lanes], other[2, :, lanes])
    own, zed, far, same, opposite = audio

    def window(i):
        pieces = [ref[b, i, :, lanes] for ref in (own, zed, far) for b in range(2)]
        return jnp.concatenate(pieces + [same[i, :, lanes], opposite[i, :, lanes]], axis=0)

    return q, k, v, window(0), window(1)


def scores_of(q, k, ka, scale, bias, rows):
    local = by_block(lambda kb, qb: dot(kb, qb, 1, 1), k, q) * scale
    audio = dot(ka, jnp.concatenate(q, axis=0), 1, 1) * scale
    return local, with_bias(audio, bias, rows)


def column_max(x):
    return jnp.max(x, axis=0, keepdims=True)


def column_sum(x):
    return jnp.sum(x, axis=0, keepdims=True)


def times_values(v, va, local, audio):
    return by_block(lambda vb, pb: dot(vb, pb, 0, 0), v, halves(local)) + dot(va, audio, 0, 0)


def teacher_kernel(dim, core, bias, scal, mine, other, *refs):
    *audio_refs, target = refs
    rows = audio_refs[0].shape[2]
    for i in range(target.shape[0]):
        lanes = slice(i * dim, (i + 1) * dim)
        q, k, v, ka, va = load_head(lanes, mine, other, audio_refs)
        local, audio = scores_of(q, k, ka, dim**-0.5, bias, rows)
        plain_max = column_max(local)
        plain = jnp.exp(local - plain_max)
        plain = (plain * (1.0 / column_sum(plain))).astype(jnp.bfloat16)
        highest = jnp.maximum(plain_max, column_max(audio))
        local = jnp.exp(local - highest)
        audio = jnp.exp(audio - highest)
        norm = 1.0 / (column_sum(local) + column_sum(audio))
        local = (local * norm).astype(jnp.bfloat16)
        audio = (audio * norm).astype(jnp.bfloat16)
        conditional = times_values(v, va, local, audio)
        unconditional = by_block(lambda vb, pb: dot(vb, pb, 0, 0), v, halves(plain))
        target[i] = unconditional + scal[0] * (conditional - unconditional)


def student_kernel(dim, core, bias, scal, mine, other, *refs):
    audio_refs, target = refs[:5], refs[5]
    grad_mine, grad_other, own_out, zed_out, far_out, opposite_out, totals = refs[6:]
    rows = audio_refs[0].shape[2]
    scale = dim**-0.5
    heads = target.shape[0]
    for i in range(heads):
        lanes = slice(i * dim, (i + 1) * dim)
        q, k, v, ka, va = load_head(lanes, mine, other, audio_refs)
        local, audio = scores_of(q, k, ka, scale, bias, rows)
        highest = jnp.maximum(column_max(local), column_max(audio))
        local = jnp.exp(local - highest)
        audio = jnp.exp(audio - highest)
        norm = 1.0 / (column_sum(local) + column_sum(audio))
        local = local * norm
        audio = audio * norm
        local_round = local.astype(jnp.bfloat16)
        audio_round = audio.astype(jnp.bfloat16)
        out = times_values(v, va, local_round, audio_round)
        factor = scal[2 + pl.program_id(0) * heads + i]
        residual = scal[1] * (out * factor - target[i])
        product = residual * out
        n = product.shape[1] // 2
        product = product[:, :n] + product[:, n:]
        totals[i] = jnp.sum(product.reshape(dim // 8, 8, n), axis=0)
        out_grad = (residual * factor).astype(jnp.bfloat16)
        row_delta = column_sum(out_grad.astype(jnp.float32) * out)
        grads = halves(out_grad)
        local_grad = by_block(lambda vb, gb: dot(vb, gb, 1, 0), v, grads)
        audio_grad = dot(va, out_grad, 1, 0)
        local_grad = (scale * local * (local_grad - row_delta)).astype(jnp.bfloat16)
        audio_grad = (scale * audio * (audio_grad - row_delta)).astype(jnp.bfloat16)
        query_grad = times_values(k, ka, local_grad, audio_grad).T.astype(jnp.bfloat16)
        vb = query_grad.shape[0] // 2
        score_halves = halves(local_grad)
        prob_halves = halves(local_round)
        for b, (ref, first) in enumerate(((grad_mine, (0,)), (grad_other, ()))):
            ref[(*first, 0, slice(None), lanes)] = query_grad[b * vb : (b + 1) * vb]
            key_grad = dot(score_halves[b], q[b], 1, 0)
            ref[(*first, 1, slice(None), lanes)] = key_grad.astype(jnp.bfloat16)
            value_grad = dot(prob_halves[b], grads[b], 1, 1)
            ref[(*first, 2, slice(None), lanes)] = value_grad.astype(jnp.bfloat16)
        audio_keys = dot(audio_grad, jnp.concatenate(q, axis=0), 1, 0)
        audio_values = dot(audio_round, out_grad, 1, 1)
        places = [(own_out, 0), (own_out, 1), (zed_out, 0), (zed_out, 1)]
        places += [(far_out, 0), (far_out, 1), (far_out, 2), (opposite_out, 0)]
        for slot, (ref, b) in enumerate(places):
            at = slice(slot * rows, (slot + 1) * rows)
            ref[b, 0, :, lanes] = audio_keys[at].astype(ref.dtype)
            ref[b, 1, :, lanes] = audio_values[at].astype(ref.dtype)


def specs(steps, width, vb, audio, which):
    smem = pl.BlockSpec(memory_space=pltpu.SMEM)
    mine = pl.BlockSpec((1, 3, vb, width), lambda h, c: (0, 0, 0, c[0] * steps + h))
    video = pl.BlockSpec((3, vb, width), lambda h, c: (0, 0, h))

    rows = audio[0].shape[2]
    pair = pl.BlockSpec((2, 2, rows, width), lambda h, c: (0, 0, 0, h))
    single = pl.BlockSpec((2, rows, width), lambda h, c: (which, 0, h))
    return [smem, smem, mine, video] + [pair] * 3 + [single] * 2


def teacher_call(core, bias, scal, mine, other, audio, head_dim):
    vb, half_width = mine.shape[2], other.shape[2]
    width = STEP_HEADS * head_dim
    steps = half_width // width
    heads = half_width // head_dim
    return pl.pallas_call(
        functools.partial(teacher_kernel, head_dim),
        grid_spec=pltpu.PrefetchScalarGridSpec(
            num_scalar_prefetch=1,
            grid=(steps,),
            in_specs=specs(steps, width, vb, audio, 0),
            out_specs=pl.BlockSpec((STEP_HEADS, head_dim, 2 * vb), lambda h, c: (h, 0, 0)),
        ),
        out_shape=jax.ShapeDtypeStruct((heads, head_dim, 2 * vb), jnp.float32),
        compiler_params=pltpu.CompilerParams(vmem_limit_bytes=VMEM),
        cost_estimate=pl.CostEstimate(
            flops=600_000_000, bytes_accessed=4_000_000, transcendentals=900_000
        ),
        name="teacher",
    )(core, bias, scal, mine, other, *audio)


def student_call(core, bias, scal, mine, other, audio, target, head_dim):
    vb, half_width = mine.shape[2], other.shape[2]
    rows = audio[0].shape[2]
    width = STEP_HEADS * head_dim
    steps = half_width // width
    in_specs = specs(steps, width, vb, audio, 1)
    heads = half_width // head_dim

    def blocks(n, dtype):
        shape = jax.ShapeDtypeStruct((n, 2, rows, half_width), dtype)
        return shape, pl.BlockSpec((n, 2, rows, width), lambda h, c: (0, 0, 0, h))

    outs = [
        (jax.ShapeDtypeStruct(mine.shape, jnp.bfloat16), in_specs[2]),
        (jax.ShapeDtypeStruct(other.shape, jnp.bfloat16), in_specs[3]),
        blocks(2, jnp.float32),
        blocks(2, jnp.float32),
        blocks(3, jnp.bfloat16),
        blocks(1, jnp.bfloat16),
        (
            jax.ShapeDtypeStruct((heads, 8, vb), jnp.float32),
            pl.BlockSpec((STEP_HEADS, 8, vb), lambda h, c: (h, 0, 0)),
        ),
    ]
    return pl.pallas_call(
        functools.partial(student_kernel, head_dim),
        grid_spec=pltpu.PrefetchScalarGridSpec(
            num_scalar_prefetch=1,
            grid=(steps,),
            in_specs=in_specs
            + [pl.BlockSpec((STEP_HEADS, head_dim, 2 * vb), lambda h, c: (h, 0, 0))],
            out_specs=[spec for _, spec in outs],
        ),
        out_shape=[shape for shape, _ in outs],
        compiler_params=pltpu.CompilerParams(vmem_limit_bytes=VMEM),
        cost_estimate=pl.CostEstimate(
            flops=900_000_000, bytes_accessed=8_000_000, transcendentals=600_000
        ),
        name="student",
    )(core, bias, scal, mine, other, *audio, target)


def swap(x, axis):
    return lax.ppermute(x, axis, [(0, 1), (1, 0)])


def everywhere(x, axes):
    n = lax.axis_size(axes)
    copies = jnp.broadcast_to(x[None], (n,) + x.shape)
    return jnp.sum(lax.all_to_all(copies, axes, 0, 0), axis=0)


def body(
    teacher_video,
    student_video,
    teacher_audio,
    student_audio,
    alignment,
    guidance_index,
    step_index,
    null_flag,
    gamma,
):
    heads = gamma.shape[1]
    width = teacher_video.shape[3]
    half_width = width // 2
    head_dim = width // heads
    half_heads = heads // 2
    tokens = teacher_video.shape[2]
    core = lax.axis_index(CORE)
    half = lax.axis_index(HALF)
    position = lax.axis_index(SEQ)
    base = position - core

    group = lax.axis_size(HALF) * lax.axis_size(CORE)
    count = lax.axis_size(SEQ)
    places = range(count)

    def inside(pairs):
        return [(a, b) for a, b in pairs if 0 <= b < count]

    far_out = inside((i, i - group if (i // 2) % 2 else i + group) for i in places)
    far_back = [(b, a) for a, b in far_out]

    def part(x, which):
        return lax.dynamic_slice_in_dim(x, which * half_width, half_width, x.ndim - 1)

    audio = jnp.concatenate([teacher_audio[0], student_audio[0]], axis=0)
    kept = part(audio, core)
    got = swap(part(audio, 1 - core), CORE)
    inner = core == half
    pairs = [jnp.stack([kept[i : i + 2], got[i : i + 2]]) for i in (0, 2)]
    zeds = [swap(pair, HALF) for pair in pairs]
    zeds[0], guidance_index, step_index = lax.optimization_barrier(
        (zeds[0], guidance_index, step_index)
    )
    same = lax.ppermute(jnp.where(inner, got, kept), SEQ, far_out)
    opposite = lax.ppermute(jnp.where(inner, kept, got), SEQ, far_back)
    same, teacher_video, student_video, alignment = lax.optimization_barrier(
        (same, teacher_video, student_video, alignment)
    )
    fars = [lax.ppermute(zed, SEQ, far_out) for zed in zeds]
    teach_other = swap(part(teacher_video[0], 1 - core), CORE)
    pupil_other = swap(part(student_video[0], 1 - core), CORE)
    spans = lax.all_gather(alignment[0, 0], CORE)

    side = 2 - 4 * half
    near = 7 * half
    owners = jnp.stack(
        [
            base + core,
            base + 1 - core,
            base + side + core,
            base + side + 1 - core,
            base - side + core,
            base - side + 1 - core,
            base - 3 + near,
            base + 4 - near,
        ]
    )
    span = jnp.where(core == 0, spans, spans[::-1])
    first, length = span[None, :, 0], span[None, :, 1]
    used = (owners[:, None] >= first) & (owners[:, None] < first + length) & (null_flag[0] == 0)
    bias = jnp.where(used, 0.0, -jnp.inf).astype(jnp.float32).reshape(2 * SLOTS)

    level_index = guidance_index[0]
    levels = jnp.arange(gamma.shape[0], dtype=jnp.int32)
    weight = 1.0 + 0.75 * level_index.astype(jnp.float32)
    loss_weight = 1.0 / (1.0 + step_index[0].astype(jnp.float32) / 250.0)
    factor = jnp.sum(
        jnp.where(levels[:, None] == level_index, gamma, jnp.zeros_like(gamma)), axis=0
    )
    factor = lax.dynamic_slice_in_dim(factor, core * half_heads, half_heads)
    scal = jnp.concatenate([jnp.stack([weight, loss_weight]), factor])
    which = core.astype(jnp.int32)[None]

    windows = [(pair, zed, far, same, opposite) for pair, zed, far in zip(pairs, zeds, fars)]
    target = teacher_call(which, bias, scal, teacher_video, teach_other, windows[0], head_dim)
    grad_video, grad_other, own, zed, far, opposite, totals = student_call(
        which, bias, scal, student_video, pupil_other, windows[1], target, head_dim
    )

    sums = jnp.sum(totals, axis=(1, 2))
    head_totals = lax.dynamic_update_slice_in_dim(
        jnp.zeros((heads,), jnp.float32), sums, core * half_heads, 0
    )
    contribution = jnp.where(
        levels[:, None] == level_index, head_totals[None, :], jnp.zeros_like(gamma)
    )
    far_in = lax.ppermute(far, SEQ, far_back)
    far_in, contribution = lax.optimization_barrier((far_in, everywhere(contribution, COLUMN)))
    far_in = far_in.astype(jnp.float32)
    opposite_in = lax.ppermute(opposite[0], SEQ, far_out).astype(jnp.float32)
    zed_in = swap((zed + far_in[:2]).astype(jnp.bfloat16), HALF)
    zed_in, gamma_grad = lax.optimization_barrier((zed_in, everywhere(contribution, PLANE)))
    zed_in = zed_in.astype(jnp.float32)
    near_in = (far_in[2], opposite_in)
    keep = own[0] + jnp.where(inner, near_in[1], near_in[0])
    leave = own[1] + jnp.where(inner, near_in[0], near_in[1])
    keep = (keep + zed_in[0]).astype(jnp.bfloat16)
    arrived = swap((leave + zed_in[1]).astype(jnp.bfloat16), CORE)
    grad_audio = jnp.where(
        core == 0,
        jnp.concatenate([keep, arrived], axis=-1),
        jnp.concatenate([arrived, keep], axis=-1),
    )[None]
    grad_video = lax.dynamic_update_slice_in_dim(
        grad_video, swap(grad_other, CORE)[None], (1 - core) * half_width, 3
    )

    gamma_grad = gamma_grad / (tokens * count * head_dim)
    return (grad_video, grad_audio, gamma_grad)


def solution(mesh):
    finer = Mesh(
        mesh.devices.reshape(8, 4, 2, 2, mesh.shape["dp"]),
        ("seq_0", "seq_1", "seq_2", "seq_3", "dp"),
    )
    in_specs = (
        P("dp", None, SEQ, None),
        P("dp", None, SEQ, None),
        P("dp", None, SEQ, None),
        P("dp", None, SEQ, None),
        P("dp", SEQ, None),
        P("dp"),
        P("dp"),
        P("dp"),
        P(),
    )
    out_specs = (P("dp", None, SEQ, None), P("dp", None, SEQ, None), P())
    return jax.shard_map(body, mesh=finer, in_specs=in_specs, out_specs=out_specs, check_vma=False)
```
